512 devices in a mesh: dp: 32 (over y, x, z_hi), land: 16 (over z_lo, core).
Axes of the slice: x: 4, y: 4, z: 16 (z_hi: 2, z_lo: 8; z = z_hi * 8 + z_lo), core: 2. Of those that a mesh axis runs over, the one named last changes fastest.
Arguments:
- embeddings: bfloat16 [16384, 4096], P('dp', 'land'), may hold values from -6 to 6
- landmarks: bfloat16 [4096, 4096], P('land', 'dp'), may hold values from -6 to 6
- alpha: float32 [4096], P('land'), may hold values from -0.09375 to 0.09375
- pairs: int32 [2, 32768], P(None, 'dp'), may hold values from 0 to 511, as said below
Outputs:
- gram: float32 [4096, 4096], P('dp', 'land')
- gradient: float32 [4096], P('land')
The draws below stay inside these ranges and needn't reach their ends.
Inputs may be any that keep to these rules, and one draw needn't show every extreme that they name: `pairs`: pairs come in blocks of 256 in each index of dp; block j of an index compares only responses j * 128 to (j + 1) * 128 - 1 of that index, and a pair's winner and loser differ.
All inputs are finite; a program needn't handle non-finite values.
Results may differ from the reference program's by a relative error of at most 0.0048.
Values may be sent and summed in bfloat16 or wider, within the bound.
No kernel may reach another device: no remote copies, remote signals or barrier semaphores. Data moves between devices by JAX's collectives and lax.ppermute only.
A program may use at most 64 MiB of HBM per device.

```python
import math
import jax
import jax.numpy as jnp
from jax import lax

EMBED_WIDTH = 4096
LANDMARKS = 4096
BLOCK_ROWS = 128
RESPONSES_DEV = 512
PAIRS_DEV = 1024
ALL_RESPONSES = 16384
ALL_PAIRS = 32768


def draw_pairs(key, part):
    key = jax.random.fold_in(key, 7)
    first_key, another_random_key = jax.random.split(key)
    index = jnp.arange(ALL_PAIRS, dtype=jnp.int32)
    local = index % PAIRS_DEV
    block = local // (2 * BLOCK_ROWS)
    position = local % (2 * BLOCK_ROWS)
    winner_local = jax.random.randint(first_key, (ALL_PAIRS,), 0, BLOCK_ROWS, dtype=jnp.int32)
    offset = jax.random.randint(another_random_key, (ALL_PAIRS,), 1, BLOCK_ROWS, dtype=jnp.int32)
    winner_local = jnp.where(position == 0, 0, winner_local)
    offset = jnp.where(position == 0, BLOCK_ROWS - 1, offset)
    loser_local = (winner_local + offset) % BLOCK_ROWS
    winners = block * BLOCK_ROWS + winner_local
    losers = block * BLOCK_ROWS + loser_local
    return jnp.stack([winners, losers]).astype(jnp.int32)


def shard_levels(stream_key, shape, cuts, low, top_value):
    gain, own = 1.0, jax.random.fold_in(stream_key, 6)
    for axis_at, blocks in cuts:
        heights = jnp.exp(jax.random.uniform(jax.random.fold_in(own, axis_at), (blocks,), jnp.float32, low / len(cuts), top_value / len(cuts)))
        gain = gain * jnp.repeat(heights, shape[axis_at] // blocks).reshape([-1 if axis == axis_at else 1 for axis in range(len(shape))])
    return gain


def gaussian(key, dims, spread, reach, cuts=(), held_as=jnp.bfloat16):
    loudness = shard_levels(key, dims, cuts, -0.22, 0.18) if cuts else 1.0
    entries = jax.random.normal(key, dims, jnp.float32) * spread * loudness
    return jnp.minimum(jnp.maximum(entries, -reach), reach).astype(held_as)


def setup_inputs(seed: int = 0) -> dict:
    streams_of = jax.random.split(jax.random.key(seed), 5)
    return {
        "embeddings": gaussian(streams_of[0], (ALL_RESPONSES, EMBED_WIDTH), 1.0, 6.0, ((0, 32), (1, 16))),
        "landmarks": gaussian(streams_of[1], (LANDMARKS, EMBED_WIDTH), 1.0, 6.0, ((0, 16), (1, 32))),
        "alpha": gaussian(streams_of[2], (LANDMARKS,), LANDMARKS ** -0.5, 0.09375, ((0, 16),), jnp.float32),
        "pairs": draw_pairs(jax.random.fold_in(streams_of[4], 71), 0),
    }


def make_features(inner, resp_square, landmark_square_norm):
    beta = 0.5 * math.sqrt(EMBED_WIDTH)
    value = beta * inner * lax.rsqrt(resp_square + 1e-06)[:, None] * lax.rsqrt(landmark_square_norm + 1e-06)[None, :]
    return jnp.exp(value).astype(jnp.bfloat16)

def reference(embeddings, landmarks, alpha, pairs):
    inner = jnp.dot(embeddings, landmarks.T, preferred_element_type=jnp.float32)
    resp_square = lax.optimization_barrier(jnp.sum(jnp.square(embeddings.astype(jnp.float32)), axis=1))
    landmark_square_norm = lax.optimization_barrier(jnp.sum(jnp.square(landmarks.astype(jnp.float32)), axis=1))
    nystrom_feature_matrix = make_features(inner, resp_square, landmark_square_norm)
    offsets = jnp.arange(ALL_PAIRS, dtype=jnp.int32) // PAIRS_DEV * RESPONSES_DEV
    winners = (pairs[0] + offsets).astype(jnp.int32)
    losers = (pairs[1] + offsets).astype(jnp.int32)
    diffs = (nystrom_feature_matrix[winners].astype(jnp.float32) - nystrom_feature_matrix[losers].astype(jnp.float32)).astype(jnp.bfloat16)
    margin = jnp.dot(diffs.astype(jnp.float32), alpha, precision=lax.Precision.HIGHEST)
    prob = jax.nn.sigmoid(margin)
    weight = prob * (1.0 - prob)
    scale = 1.0 / math.sqrt(ALL_PAIRS)
    weighted = (diffs.astype(jnp.float32) * (weight * scale)[:, None]).astype(jnp.bfloat16)
    gram = jnp.dot(diffs.T, weighted, preferred_element_type=jnp.float32)
    gradient = jnp.dot((1.0 - prob) * scale, diffs.astype(jnp.float32), precision=lax.Precision.HIGHEST)
    return (gram, gradient)
```

```python
import functools
import math

import jax
import jax.numpy as jnp
from jax import lax
from jax.experimental import pallas as pl
from jax.experimental.pallas import tpu as pltpu
from jax.sharding import Mesh, PartitionSpec as P

EMBED_WIDTH = 4096
BLOCK_ROWS = 128
BETA = 0.5 * math.sqrt(EMBED_WIDTH)
LINE = ("zh", "zl", "c")
PLANE = ("y", "x")
NT = (((1,), (1,)), ((), ()))


def features_kernel(emb_ref, land_ref, out_ref, acc, resp_sq, land_sq):
    step = pl.program_id(1)
    emb, land = emb_ref[...], land_ref[...]

    @pl.when(step == 0)
    def _():
        acc[...] = jnp.zeros_like(acc)
        resp_sq[...] = jnp.zeros_like(resp_sq)
        land_sq[...] = jnp.zeros_like(land_sq)

    acc[...] += lax.dot_general(land, emb, NT, preferred_element_type=jnp.float32)
    for sums, values in ((resp_sq, emb), (land_sq, land)):
        total = sums[...]
        for at in range(0, values.shape[1], 128):
            part = values[:, at : at + 128].astype(jnp.float32)
            total += part * part
        sums[...] = total

    @pl.when(step == pl.num_programs(1) - 1)
    def _():
        ones = jnp.ones((8, 128), jnp.float32)
        resp = lax.dot_general(
            ones, resp_sq[...], NT, precision=lax.Precision.HIGHEST, preferred_element_type=jnp.float32
        )[0:1]
        norm = jnp.sum(land_sq[...], axis=1, keepdims=True)
        value = BETA * acc[...] * lax.rsqrt(resp + 1e-06) * lax.rsqrt(norm + 1e-06)
        out_ref[...] = jnp.exp(value).astype(out_ref.dtype)


def make_features(emb, land, slabs, rows):
    count, width = land.shape
    tile = 1024
    steps = width // tile
    return pl.pallas_call(
        features_kernel,
        grid=(slabs, steps),
        in_specs=[
            pl.BlockSpec((rows, tile), lambda s, k: (0, s * steps + k)),
            pl.BlockSpec((count, tile), lambda s, k: (0, k)),
        ],
        out_specs=pl.BlockSpec((count, rows), lambda s, k: (0, s)),
        out_shape=jax.ShapeDtypeStruct((count, slabs * rows), jnp.bfloat16),
        scratch_shapes=[
            pltpu.VMEM((count, rows), jnp.float32),
            pltpu.VMEM((rows, 128), jnp.float32),
            pltpu.VMEM((count, 128), jnp.float32),
        ],
        compiler_params=pltpu.CompilerParams(vmem_limit_bytes=32 * 1024 * 1024),
        cost_estimate=pl.CostEstimate(
            flops=2 * count * slabs * rows * width,
            bytes_accessed=2 * slabs * rows * width,
            transcendentals=count * slabs * rows,
        ),
    )(emb, land)


def gram_kernel(scale, at_ref, feat_ref, alpha_ref, row_ref, col_ref, out_ref, v_ref):
    half, own = at_ref[0], at_ref[1]
    count, responses = feat_ref.shape
    blocks = responses // BLOCK_ROWS
    pairs = 2 * BLOCK_ROWS
    slab_blocks = blocks // 2
    alpha = alpha_ref[...]
    high = alpha.astype(jnp.bfloat16).astype(jnp.float32)
    middle = (alpha - high).astype(jnp.bfloat16).astype(jnp.float32)
    low = alpha - high - middle
    row = lax.broadcasted_iota(jnp.int32, (16, count), 0)
    split = jnp.where(row == 0, high, jnp.where(row == 1, middle, jnp.where(row == 2, low, 0.0)))
    scores = jnp.dot(split.astype(jnp.bfloat16), feat_ref[...], preferred_element_type=jnp.float32)
    scores = scores[0:1] + scores[1:2] + scores[2:3]

    first = pl.multiple_of(own * BLOCK_ROWS, BLOCK_ROWS)
    second = pl.multiple_of(count // 2 + own * BLOCK_ROWS, BLOCK_ROWS)
    grad = jnp.zeros((1, pairs), jnp.float32)
    lane = lax.broadcasted_iota(jnp.int32, (pairs, BLOCK_ROWS), 1)
    sub = lax.broadcasted_iota(jnp.int32, (BLOCK_ROWS, pairs), 0)
    for b in range(blocks):
        base = (b % slab_blocks) * BLOCK_ROWS
        cols = slice(b * BLOCK_ROWS, (b + 1) * BLOCK_ROWS)
        select = jnp.where(col_ref[b, :, 0:1] - base == lane, 1.0, 0.0) - jnp.where(
            col_ref[b, :, 1:2] - base == lane, 1.0, 0.0
        )
        margin = jnp.sum(select * scores[:, cols], axis=1, keepdims=True)
        prob = 1.0 / (1.0 + jnp.exp(-margin))
        weight = prob * (1.0 - prob) * scale
        features = jnp.concatenate(
            [feat_ref[pl.ds(first, BLOCK_ROWS), cols], feat_ref[pl.ds(second, BLOCK_ROWS), cols]], axis=0
        )
        diffs = lax.dot_general(
            select.astype(jnp.bfloat16), features, NT, preferred_element_type=jnp.float32
        )
        diffs = diffs.astype(jnp.bfloat16).astype(jnp.float32)
        weighted = (diffs * weight).astype(jnp.bfloat16)
        grad += jnp.sum(diffs * ((1.0 - prob) * scale), axis=0, keepdims=True)
        back = jnp.where(row_ref[b, 0:1, :] - base == sub, 1.0, 0.0) - jnp.where(
            row_ref[b, 1:2, :] - base == sub, 1.0, 0.0
        )
        v = jnp.dot(back.astype(jnp.bfloat16), weighted, preferred_element_type=jnp.float32)
        v_high = v.astype(jnp.bfloat16)
        v_ref[cols, 0:pairs] = v_high
        v_ref[cols, pairs : 2 * pairs] = (v - v_high.astype(jnp.float32)).astype(jnp.bfloat16)

    grad_high = grad.astype(jnp.bfloat16).astype(jnp.float32)
    tail_row = lax.broadcasted_iota(jnp.int32, (16, pairs), 0)
    tail = jnp.where(tail_row == 0, grad_high, jnp.where(tail_row == 1, grad - grad_high, 0.0))
    tail = tail.astype(jnp.bfloat16)
    v = v_ref[...]

    def block(d, _):
        at = pl.multiple_of(half * (count // 2) + d * BLOCK_ROWS, BLOCK_ROWS)
        part = jnp.dot(feat_ref[pl.ds(at, BLOCK_ROWS), :], v_ref[...], preferred_element_type=jnp.float32)
        out_ref[d, 0:BLOCK_ROWS, :] = (part[:, 0:pairs] + part[:, pairs:]).astype(jnp.bfloat16)
        out_ref[d, BLOCK_ROWS:, :] = tail
        return 0

    lax.fori_loop(0, out_ref.shape[0], block, 0)


def make_gram(at, features, alpha, row_pairs, col_pairs, scale, owners):
    count, responses = features.shape
    vmem = pl.BlockSpec(memory_space=pltpu.VMEM)
    return pl.pallas_call(
        functools.partial(gram_kernel, scale),
        in_specs=[pl.BlockSpec(memory_space=pltpu.SMEM), vmem, vmem, vmem, vmem],
        out_specs=vmem,
        out_shape=jax.ShapeDtypeStruct((owners, BLOCK_ROWS + 16, 2 * BLOCK_ROWS), jnp.bfloat16),
        scratch_shapes=[pltpu.VMEM((responses, 4 * BLOCK_ROWS), jnp.bfloat16)],
        compiler_params=pltpu.CompilerParams(vmem_limit_bytes=40 * 1024 * 1024),
        cost_estimate=pl.CostEstimate(
            flops=2 * count * responses * 256, bytes_accessed=2 * count * responses, transcendentals=2048
        ),
    )(at, features, alpha, row_pairs, col_pairs)


def per_device(embeddings, landmarks, alpha, pairs):
    rows, pair_count = embeddings.shape[0], pairs.shape[1]
    planes = lax.axis_size(PLANE)
    slabs = lax.axis_size("zh")
    scale = 1.0 / math.sqrt(pair_count * slabs * planes)
    zh = lax.axis_index("zh")
    own = lax.axis_index(("zl", "c"))

    emb = lax.all_gather(embeddings, LINE, axis=1, tiled=True)

    half = landmarks.shape[0] // slabs
    spread = jnp.broadcast_to(
        landmarks.reshape(1, slabs, half, landmarks.shape[1]), (planes, slabs, half, landmarks.shape[1])
    ).reshape(planes * slabs * half, landmarks.shape[1])
    land = lax.all_to_all(spread, PLANE + ("zh",), 0, 0, tiled=True)
    land = land.reshape(planes * slabs, half, -1).transpose(1, 0, 2).reshape(half, -1)

    lands = lax.axis_size(("zl", "c"))
    alphas = lax.all_to_all(jnp.broadcast_to(alpha[None], (lands, alpha.shape[0])), ("zl", "c"), 0, 0, tiled=True)
    alphas = alphas.reshape(lands, slabs, half).transpose(1, 0, 2).reshape(1, -1)

    other = lax.ppermute(pairs, "zh", [(0, 1), (1, 0)])
    both = jnp.where(zh == 0, jnp.stack([pairs, other]), jnp.stack([other, pairs]))
    blocks = slabs * rows // BLOCK_ROWS
    row_pairs = both.reshape(slabs, 2, blocks // slabs, -1).transpose(0, 2, 1, 3).reshape(blocks, 2, -1)
    col_pairs = row_pairs.transpose(0, 2, 1)

    mine = make_features(emb, land, slabs, rows)
    features = lax.all_gather(mine, LINE, axis=0, tiled=True)
    at = jnp.stack([zh, own]).astype(jnp.int32)
    parts = make_gram(at, features, alphas, row_pairs, col_pairs, scale, planes)
    parts = lax.all_to_all(parts, PLANE, 0, 0, tiled=True)
    total = jnp.sum(parts.astype(jnp.float32), axis=0)
    return total[:BLOCK_ROWS], total[BLOCK_ROWS] + total[BLOCK_ROWS + 1]


def solution(mesh):
    fine = Mesh(mesh.devices.reshape(4, 4, 2, 8, 2), ("y", "x", "zh", "zl", "c"))
    dp, land = ("y", "x", "zh"), ("zl", "c")
    return jax.shard_map(
        per_device,
        mesh=fine,
        in_specs=(P(dp, land), P(land, dp), P(land), P(None, dp)),
        out_specs=(P(dp, land), P(land)),
        check_vma=False,
    )
```

```python
import functools
import math

import jax
import jax.numpy as jnp
from jax import lax
from jax.experimental import pallas as pl
from jax.experimental.pallas import tpu as pltpu
from jax.sharding import Mesh, PartitionSpec as P

EMBED_WIDTH = 4096
BLOCK_ROWS = 128
BETA = 0.5 * math.sqrt(EMBED_WIDTH)
LINE = ("zh", "zl", "c")
PLANE = ("y", "x")
NT = (((1,), (1,)), ((), ()))


def features_kernel(emb_ref, land_ref, out_ref, acc, resp_sq, land_sq):
    step = pl.program_id(1)

    @pl.when(step == 0)
    def _():
        acc[...] = jnp.zeros_like(acc)
        resp_sq[...] = jnp.zeros_like(resp_sq)
        land_sq[...] = jnp.zeros_like(land_sq)

    acc[...] += lax.dot_general(emb_ref[...], land_ref[...], NT, preferred_element_type=jnp.float32)
    for sums, ref in ((resp_sq, emb_ref), (land_sq, land_ref)):
        total = sums[...]
        for at in range(0, ref.shape[1], 128):
            part = ref[:, at : at + 128].astype(jnp.float32)
            total += part * part
        sums[...] = total

    @pl.when(step == pl.num_programs(1) - 1)
    def _():
        ones = jnp.ones((8, 128), jnp.float32)
        norm = lax.dot_general(
            ones, land_sq[...], NT, precision=lax.Precision.HIGHEST, preferred_element_type=jnp.float32
        )[0:1]
        resp = jnp.sum(resp_sq[...], axis=1, keepdims=True)
        value = BETA * acc[...] * lax.rsqrt(resp + 1e-06) * lax.rsqrt(norm + 1e-06)
        out_ref[...] = jnp.exp(value).T.astype(out_ref.dtype)


def make_features(emb, land, slabs, rows):
    count, width = land.shape
    tile = 1024
    steps = width // tile
    return pl.pallas_call(
        features_kernel,
        grid=(slabs, steps),
        in_specs=[
            pl.BlockSpec((rows, tile), lambda s, k: (0, s * steps + k)),
            pl.BlockSpec((count, tile), lambda s, k: (0, k)),
        ],
        out_specs=pl.BlockSpec((count, rows), lambda s, k: (0, s)),
        out_shape=jax.ShapeDtypeStruct((count, slabs * rows), jnp.bfloat16),
        scratch_shapes=[
            pltpu.VMEM((rows, count), jnp.float32),
            pltpu.VMEM((rows, 128), jnp.float32),
            pltpu.VMEM((count, 128), jnp.float32),
        ],
        compiler_params=pltpu.CompilerParams(vmem_limit_bytes=60 * 1024 * 1024),
        cost_estimate=pl.CostEstimate(
            flops=2 * count * slabs * rows * width,
            bytes_accessed=2 * slabs * rows * width,
            transcendentals=count * slabs * rows,
        ),
    )(emb, land)


def gram_kernel(scale, at_ref, feat_ref, alpha_ref, row_ref, col_ref, out_ref, v_ref):
    half, own = at_ref[0], at_ref[1]
    count, responses = feat_ref.shape
    blocks = responses // BLOCK_ROWS
    pairs = 2 * BLOCK_ROWS
    slab_blocks = blocks // 2
    alpha = alpha_ref[...]
    high = alpha.astype(jnp.bfloat16).astype(jnp.float32)
    middle = (alpha - high).astype(jnp.bfloat16).astype(jnp.float32)
    low = alpha - high - middle
    row = lax.broadcasted_iota(jnp.int32, (16, count), 0)
    split = jnp.where(row == 0, high, jnp.where(row == 1, middle, jnp.where(row == 2, low, 0.0)))
    scores = jnp.dot(split.astype(jnp.bfloat16), feat_ref[...], preferred_element_type=jnp.float32)
    scores = scores[0:1] + scores[1:2] + scores[2:3]

    first = pl.multiple_of(own * BLOCK_ROWS, BLOCK_ROWS)
    second = pl.multiple_of(count // 2 + own * BLOCK_ROWS, BLOCK_ROWS)
    grad = jnp.zeros((1, pairs), jnp.float32)
    lane = lax.broadcasted_iota(jnp.int32, (pairs, BLOCK_ROWS), 1)
    sub = lax.broadcasted_iota(jnp.int32, (BLOCK_ROWS, pairs), 0)
    for b in range(blocks):
        base = (b % slab_blocks) * BLOCK_ROWS
        cols = slice(b * BLOCK_ROWS, (b + 1) * BLOCK_ROWS)
        select = jnp.where(col_ref[b, :, 0:1] - base == lane, 1.0, 0.0) - jnp.where(
            col_ref[b, :, 1:2] - base == lane, 1.0, 0.0
        )
        margin = jnp.sum(select * scores[:, cols], axis=1, keepdims=True)
        prob = 1.0 / (1.0 + jnp.exp(-margin))
        weight = prob * (1.0 - prob) * scale
        features = jnp.concatenate(
            [feat_ref[pl.ds(first, BLOCK_ROWS), cols], feat_ref[pl.ds(second, BLOCK_ROWS), cols]], axis=0
        )
        diffs = lax.dot_general(
            select.astype(jnp.bfloat16), features, NT, preferred_element_type=jnp.float32
        )
        diffs = diffs.astype(jnp.bfloat16).astype(jnp.float32)
        weighted = (diffs * weight).astype(jnp.bfloat16)
        grad += jnp.sum(diffs * ((1.0 - prob) * scale), axis=0, keepdims=True)
        back = jnp.where(row_ref[b, 0:1, :] - base == sub, 1.0, 0.0) - jnp.where(
            row_ref[b, 1:2, :] - base == sub, 1.0, 0.0
        )
        v = jnp.dot(back.astype(jnp.bfloat16), weighted, preferred_element_type=jnp.float32)
        v_high = v.astype(jnp.bfloat16)
        v_ref[cols, 0:pairs] = v_high
        v_ref[cols, pairs : 2 * pairs] = (v - v_high.astype(jnp.float32)).astype(jnp.bfloat16)

    grad_high = grad.astype(jnp.bfloat16).astype(jnp.float32)
    tail_row = lax.broadcasted_iota(jnp.int32, (16, pairs), 0)
    tail = jnp.where(tail_row == 0, grad_high, jnp.where(tail_row == 1, grad - grad_high, 0.0))
    tail = tail.astype(jnp.bfloat16)

    def block(d, _):
        at = pl.multiple_of(half * (count // 2) + d * BLOCK_ROWS, BLOCK_ROWS)
        part = jnp.dot(feat_ref[pl.ds(at, BLOCK_ROWS), :], v_ref[...], preferred_element_type=jnp.float32)
        out_ref[d, 0:BLOCK_ROWS, :] = (part[:, 0:pairs] + part[:, pairs:]).astype(jnp.bfloat16)
        out_ref[d, BLOCK_ROWS:, :] = tail
        return 0

    lax.fori_loop(0, out_ref.shape[0], block, 0)


def make_gram(at, features, alpha, row_pairs, col_pairs, scale, owners):
    count, responses = features.shape
    vmem = pl.BlockSpec(memory_space=pltpu.VMEM)
    return pl.pallas_call(
        functools.partial(gram_kernel, scale),
        in_specs=[pl.BlockSpec(memory_space=pltpu.SMEM), vmem, vmem, vmem, vmem],
        out_specs=vmem,
        out_shape=jax.ShapeDtypeStruct((owners, BLOCK_ROWS + 16, 2 * BLOCK_ROWS), jnp.bfloat16),
        scratch_shapes=[pltpu.VMEM((responses, 4 * BLOCK_ROWS), jnp.bfloat16)],
        compiler_params=pltpu.CompilerParams(vmem_limit_bytes=60 * 1024 * 1024),
        cost_estimate=pl.CostEstimate(
            flops=2 * count * responses * 256, bytes_accessed=2 * count * responses, transcendentals=2048
        ),
    )(at, features, alpha, row_pairs, col_pairs)


def per_device(embeddings, landmarks, alpha, pairs):
    rows, pair_count = embeddings.shape[0], pairs.shape[1]
    planes = lax.axis_size(PLANE)
    slabs = lax.axis_size("zh")
    scale = 1.0 / math.sqrt(pair_count * slabs * planes)
    zh = lax.axis_index("zh")
    own = lax.axis_index(("zl", "c"))

    emb = lax.all_gather(embeddings, LINE, axis=1, tiled=True)

    half = landmarks.shape[0] // slabs
    halves = landmarks.reshape(slabs, half, landmarks.shape[1])
    kept, sent = jnp.where(zh == 0, halves, halves[::-1])
    came = lax.ppermute(sent, "zh", [(0, 1), (1, 0)])
    part = jnp.where(zh == 0, jnp.concatenate([kept, came], axis=1), jnp.concatenate([came, kept], axis=1))
    spread = jnp.broadcast_to(part[None], (planes,) + part.shape).reshape(planes * half, -1)
    land = lax.all_to_all(spread, PLANE, 0, 0, tiled=True)
    land = land.reshape(planes, half, -1).transpose(1, 0, 2).reshape(half, -1)

    lands = lax.axis_size(("zl", "c"))
    alphas = lax.all_to_all(jnp.broadcast_to(alpha[None], (lands, alpha.shape[0])), ("zl", "c"), 0, 0, tiled=True)
    alphas = alphas.reshape(lands, slabs, half).transpose(1, 0, 2).reshape(1, -1)

    other = lax.ppermute(pairs, "zh", [(0, 1), (1, 0)])
    both = jnp.where(zh == 0, jnp.stack([pairs, other]), jnp.stack([other, pairs]))
    blocks = slabs * rows // BLOCK_ROWS
    row_pairs = both.reshape(slabs, 2, blocks // slabs, -1).transpose(0, 2, 1, 3).reshape(blocks, 2, -1)
    col_pairs = row_pairs.transpose(0, 2, 1)

    mine = make_features(emb, land, slabs, rows)
    features = lax.all_gather(mine, LINE, axis=0, tiled=True)
    at = jnp.stack([zh, own]).astype(jnp.int32)
    parts = make_gram(at, features, alphas, row_pairs, col_pairs, scale, planes)
    parts = lax.all_to_all(parts, PLANE, 0, 0, tiled=True)
    total = jnp.sum(parts.astype(jnp.float32), axis=0)
    return total[:BLOCK_ROWS], total[BLOCK_ROWS] + total[BLOCK_ROWS + 1]


def solution(mesh):
    fine = Mesh(mesh.devices.reshape(4, 4, 2, 8, 2), ("y", "x", "zh", "zl", "c"))
    dp, land = ("y", "x", "zh"), ("zl", "c")
    return jax.shard_map(
        per_device,
        mesh=fine,
        in_specs=(P(dp, land), P(land, dp), P(land), P(None, dp)),
        out_specs=(P(dp, land), P(land)),
        check_vma=False,
    )
```

```python
import functools
import math

import jax
import jax.numpy as jnp
from jax import lax
from jax.experimental import pallas as pl
from jax.experimental.pallas import tpu as pltpu
from jax.sharding import Mesh, PartitionSpec as P

EMBED_WIDTH = 4096
BLOCK_ROWS = 128
BETA = 0.5 * math.sqrt(EMBED_WIDTH)
LINE = ("zh", "zl", "c")
PLANE = ("y", "x")
NT = (((1,), (1,)), ((), ()))


def features_kernel(emb_ref, land_ref, alpha_ref, out_ref, score_ref, acc, resp_sq, land_sq):
    step = pl.program_id(1)
    chunks, _, width = emb_ref.shape

    @pl.when(step == 0)
    def _():
        acc[...] = jnp.zeros_like(acc)
        resp_sq[...] = jnp.zeros_like(resp_sq)
        land_sq[...] = jnp.zeros_like(land_sq)

    total = acc[...]
    resp, land = resp_sq[...], land_sq[...]
    for j in range(chunks):
        cols = slice(j * width, (j + 1) * width)
        total += lax.dot_general(emb_ref[j], land_ref[:, cols], NT, preferred_element_type=jnp.float32)
        for at in range(0, width, 128):
            part = emb_ref[j, :, at : at + 128].astype(jnp.float32)
            resp += part * part
            part = land_ref[:, j * width + at : j * width + at + 128].astype(jnp.float32)
            land += part * part
    acc[...] = total
    resp_sq[...] = resp
    land_sq[...] = land

    @pl.when(step == pl.num_programs(1) - 1)
    def _():
        ones = jnp.ones((8, 128), jnp.float32)
        norm = lax.dot_general(
            ones, land_sq[...], NT, precision=lax.Precision.HIGHEST, preferred_element_type=jnp.float32
        )[0:1]
        square = jnp.sum(resp_sq[...], axis=1, keepdims=True)
        value = BETA * acc[...] * lax.rsqrt(square + 1e-06) * lax.rsqrt(norm + 1e-06)
        features = jnp.exp(value).T.astype(out_ref.dtype)
        out_ref[...] = features
        score_ref[...] = jnp.sum(features.astype(jnp.float32) * alpha_ref[...], axis=0, keepdims=True)


def make_features(emb, land, alpha, slabs):
    chunks, rows, part = emb.shape
    count, width = land.shape
    steps = 1
    tile = width // steps
    each = tile // part
    return pl.pallas_call(
        features_kernel,
        grid=(slabs, steps),
        in_specs=[
            pl.BlockSpec((each, rows, part), lambda s, k: (s * steps + k, 0, 0)),
            pl.BlockSpec((count, tile), lambda s, k: (0, k)),
            pl.BlockSpec((count, 1), lambda s, k: (0, 0)),
        ],
        out_specs=[
            pl.BlockSpec((count, rows), lambda s, k: (0, s)),
            pl.BlockSpec((1, rows), lambda s, k: (0, s)),
        ],
        out_shape=[
            jax.ShapeDtypeStruct((count, slabs * rows), jnp.bfloat16),
            jax.ShapeDtypeStruct((1, slabs * rows), jnp.float32),
        ],
        scratch_shapes=[
            pltpu.VMEM((rows, count), jnp.float32),
            pltpu.VMEM((rows, 128), jnp.float32),
            pltpu.VMEM((count, 128), jnp.float32),
        ],
        compiler_params=pltpu.CompilerParams(vmem_limit_bytes=60 * 1024 * 1024),
        cost_estimate=pl.CostEstimate(
            flops=2 * count * slabs * rows * width,
            bytes_accessed=2 * slabs * rows * width,
            transcendentals=count * slabs * rows,
        ),
    )(emb, land, alpha)


def gram_kernel(scale, at_ref, feat_ref, score_ref, row_ref, col_ref, out_ref, own_ref, half_ref, v_ref, sems):
    half, own = at_ref[0], at_ref[1]
    count, responses = feat_ref.shape
    blocks = responses // BLOCK_ROWS
    pairs = 2 * BLOCK_ROWS
    slab_blocks = blocks // 2
    copies = []
    for k in range(2):
        rows = pl.ds(pl.multiple_of(k * (count // 2) + own * BLOCK_ROWS, BLOCK_ROWS), BLOCK_ROWS)
        copies.append(
            pltpu.make_async_copy(feat_ref.at[rows], own_ref.at[pl.ds(k * BLOCK_ROWS, BLOCK_ROWS)], sems.at[k])
        )
    rows = pl.ds(pl.multiple_of(half * (count // 2), BLOCK_ROWS), count // 2)
    copies.append(pltpu.make_async_copy(feat_ref.at[rows], half_ref, sems.at[2]))
    for copy in copies:
        copy.start()
    scores = jnp.sum(score_ref[...], axis=0, keepdims=True)
    copies[0].wait()
    copies[1].wait()

    grad = jnp.zeros((1, pairs), jnp.float32)
    lane = lax.broadcasted_iota(jnp.int32, (pairs, BLOCK_ROWS), 1)
    sub = lax.broadcasted_iota(jnp.int32, (BLOCK_ROWS, pairs), 0)
    for b in range(blocks):
        base = (b % slab_blocks) * BLOCK_ROWS
        cols = slice(b * BLOCK_ROWS, (b + 1) * BLOCK_ROWS)
        select = jnp.where(col_ref[b, :, 0:1] - base == lane, 1.0, 0.0) - jnp.where(
            col_ref[b, :, 1:2] - base == lane, 1.0, 0.0
        )
        margin = jnp.sum(select * scores[:, cols], axis=1, keepdims=True)
        prob = 1.0 / (1.0 + jnp.exp(-margin))
        weight = prob * (1.0 - prob) * scale
        diffs = lax.dot_general(
            select.astype(jnp.bfloat16), own_ref[:, cols], NT, preferred_element_type=jnp.float32
        )
        diffs = diffs.astype(jnp.bfloat16).astype(jnp.float32)
        weighted = (diffs * weight).astype(jnp.bfloat16)
        grad += jnp.sum(diffs * ((1.0 - prob) * scale), axis=0, keepdims=True)
        back = jnp.where(row_ref[b, 0:1, :] - base == sub, 1.0, 0.0) - jnp.where(
            row_ref[b, 1:2, :] - base == sub, 1.0, 0.0
        )
        v = jnp.dot(back.astype(jnp.bfloat16), weighted, preferred_element_type=jnp.float32)
        v_high = v.astype(jnp.bfloat16)
        v_ref[cols, 0:pairs] = v_high
        v_ref[cols, pairs : 2 * pairs] = (v - v_high.astype(jnp.float32)).astype(jnp.bfloat16)

    grad_high = grad.astype(jnp.bfloat16).astype(jnp.float32)
    tail_row = lax.broadcasted_iota(jnp.int32, (16, pairs), 0)
    tail = jnp.where(tail_row == 0, grad_high, jnp.where(tail_row == 1, grad - grad_high, 0.0))
    tail = tail.astype(jnp.bfloat16)
    copies[2].wait()
    for d in range(0, out_ref.shape[0], 2):
        part = jnp.dot(
            half_ref[d * BLOCK_ROWS : (d + 2) * BLOCK_ROWS, :], v_ref[...], preferred_element_type=jnp.float32
        )
        part = (part[:, 0:pairs] + part[:, pairs:]).astype(jnp.bfloat16)
        for k in range(2):
            out_ref[d + k, 0:BLOCK_ROWS, :] = part[k * BLOCK_ROWS : (k + 1) * BLOCK_ROWS]
            out_ref[d + k, BLOCK_ROWS:, :] = tail


def make_gram(at, features, scores, row_pairs, col_pairs, scale, owners):
    count, responses = features.shape
    vmem = pl.BlockSpec(memory_space=pltpu.VMEM)
    return pl.pallas_call(
        functools.partial(gram_kernel, scale),
        in_specs=[
            pl.BlockSpec(memory_space=pltpu.SMEM),
            pl.BlockSpec(memory_space=pl.ANY),
            vmem,
            vmem,
            vmem,
        ],
        out_specs=vmem,
        out_shape=jax.ShapeDtypeStruct((owners, BLOCK_ROWS + 16, 2 * BLOCK_ROWS), jnp.bfloat16),
        scratch_shapes=[
            pltpu.VMEM((2 * BLOCK_ROWS, responses), jnp.bfloat16),
            pltpu.VMEM((count // 2, responses), jnp.bfloat16),
            pltpu.VMEM((responses, 4 * BLOCK_ROWS), jnp.bfloat16),
            pltpu.SemaphoreType.DMA((3,)),
        ],
        compiler_params=pltpu.CompilerParams(vmem_limit_bytes=60 * 1024 * 1024),
        cost_estimate=pl.CostEstimate(
            flops=2 * count * responses * 256, bytes_accessed=count * responses, transcendentals=2048
        ),
    )(at, features, scores, row_pairs, col_pairs)


def per_device(embeddings, landmarks, alpha, pairs):
    rows, pair_count = embeddings.shape[0], pairs.shape[1]
    planes = lax.axis_size(PLANE)
    slabs = lax.axis_size("zh")
    scale = 1.0 / math.sqrt(pair_count * slabs * planes)
    zh = lax.axis_index("zh")
    own = lax.axis_index(("zl", "c"))

    emb = lax.all_gather(embeddings, LINE)

    half = landmarks.shape[0] // slabs
    halves = landmarks.reshape(slabs, half, landmarks.shape[1])
    kept, sent = jnp.where(zh == 0, halves, halves[::-1])
    came = lax.ppermute(sent, "zh", [(0, 1), (1, 0)])
    part = jnp.where(zh == 0, jnp.concatenate([kept, came], axis=1), jnp.concatenate([came, kept], axis=1))
    spread = jnp.broadcast_to(part[None], (planes,) + part.shape).reshape(planes * half, -1)
    land = lax.all_to_all(spread, PLANE, 0, 0, tiled=True)
    land = land.reshape(planes, half, -1).transpose(1, 0, 2).reshape(half, -1)

    other = lax.ppermute(pairs, "zh", [(0, 1), (1, 0)])
    both = jnp.where(zh == 0, jnp.stack([pairs, other]), jnp.stack([other, pairs]))
    blocks = slabs * rows // BLOCK_ROWS
    row_pairs = both.reshape(slabs, 2, blocks // slabs, -1).transpose(0, 2, 1, 3).reshape(blocks, 2, -1)
    col_pairs = row_pairs.transpose(0, 2, 1)

    own_alpha = jnp.where(zh == 0, alpha[:half], alpha[half:])[:, None]
    mine, score = make_features(emb, land, own_alpha, slabs)
    features = lax.all_gather(mine, LINE, axis=0, tiled=True)
    line = lax.axis_size(LINE)
    scores = lax.all_to_all(jnp.broadcast_to(score, (line, score.shape[1])), LINE, 0, 0, tiled=True)
    at = jnp.stack([zh, own]).astype(jnp.int32)
    parts = make_gram(at, features, scores, row_pairs, col_pairs, scale, planes)
    parts = lax.all_to_all(parts, PLANE, 0, 0, tiled=True)
    total = jnp.sum(parts.astype(jnp.float32), axis=0)
    return total[:BLOCK_ROWS], total[BLOCK_ROWS] + total[BLOCK_ROWS + 1]


def solution(mesh):
    fine = Mesh(mesh.devices.reshape(4, 4, 2, 8, 2), ("y", "x", "zh", "zl", "c"))
    dp, land = ("y", "x", "zh"), ("zl", "c")
    return jax.shard_map(
        per_device,
        mesh=fine,
        in_specs=(P(dp, land), P(land, dp), P(land), P(None, dp)),
        out_specs=(P(dp, land), P(land)),
        check_vma=False,
    )
```

```python
import functools
import math

import jax
import jax.numpy as jnp
from jax import lax
from jax.experimental import pallas as pl
from jax.experimental.pallas import tpu as pltpu
from jax.sharding import Mesh, PartitionSpec as P

EMBED_WIDTH = 4096
BLOCK_ROWS = 128
BETA = 0.5 * math.sqrt(EMBED_WIDTH)
RING = ("zh", "zm", "c")
PLANE = ("y", "x")
NT = (((1,), (1,)), ((), ()))


def features_kernel(emb_ref, land_ref, alpha_ref, out_ref, score_ref):
    chunks, rows, width = emb_ref.shape
    count = land_ref.shape[1]
    total = jnp.zeros((rows, count), jnp.float32)
    resp = jnp.zeros((rows, 128), jnp.float32)
    land = jnp.zeros((count, 128), jnp.float32)
    for j in range(chunks):
        zm, c, zp = j // 4, j // 2 % 2, j % 2
        at = zm * 4 + zp * 2 + c
        total += lax.dot_general(emb_ref[j], land_ref[at], NT, preferred_element_type=jnp.float32)
        for lane in range(0, width, 128):
            part = emb_ref[j, :, lane : lane + 128].astype(jnp.float32)
            resp += part * part
            part = land_ref[at, :, lane : lane + 128].astype(jnp.float32)
            land += part * part
    ones = jnp.ones((8, 128), jnp.float32)
    norm = lax.dot_general(ones, land, NT, precision=lax.Precision.HIGHEST, preferred_element_type=jnp.float32)[0:1]
    square = jnp.sum(resp, axis=1, keepdims=True)
    value = BETA * total * lax.rsqrt(square + 1e-06) * lax.rsqrt(norm + 1e-06)
    features = jnp.exp(value).T.astype(out_ref.dtype)
    out_ref[...] = features
    score_ref[...] = jnp.sum(features.astype(jnp.float32) * alpha_ref[...], axis=0, keepdims=True)


def make_features(emb, land, alpha, slabs):
    chunks, rows, part = emb.shape
    count = land.shape[1]
    each = chunks // slabs
    return pl.pallas_call(
        features_kernel,
        grid=(slabs,),
        in_specs=[
            pl.BlockSpec((each, rows, part), lambda s: (s, 0, 0)),
            pl.BlockSpec(land.shape, lambda s: (0, 0, 0)),
            pl.BlockSpec((count, 1), lambda s: (0, 0)),
        ],
        out_specs=[
            pl.BlockSpec((count, rows), lambda s: (0, s)),
            pl.BlockSpec((1, rows), lambda s: (0, s)),
        ],
        out_shape=[
            jax.ShapeDtypeStruct((count, slabs * rows), jnp.bfloat16),
            jax.ShapeDtypeStruct((1, slabs * rows), jnp.float32),
        ],
        compiler_params=pltpu.CompilerParams(vmem_limit_bytes=60 * 1024 * 1024),
        cost_estimate=pl.CostEstimate(
            flops=2 * count * chunks * rows * part,
            bytes_accessed=2 * chunks * rows * part,
            transcendentals=count * slabs * rows,
        ),
    )(emb, land, alpha)


def gram_kernel(scale, at_ref, feat_ref, score_ref, row_ref, col_ref, out_ref, own_ref, half_ref, v_ref, sems):
    half, own = at_ref[0], at_ref[1]
    count, responses = feat_ref.shape
    blocks = responses // BLOCK_ROWS
    pairs = 2 * BLOCK_ROWS
    wide = 4 * BLOCK_ROWS
    copies = []
    for k in range(4):
        zp, zh = k // 2, k % 2
        rows = pl.ds(
            pl.multiple_of(zh * (count // 2) + own * pairs + zp * BLOCK_ROWS, BLOCK_ROWS), BLOCK_ROWS
        )
        copies.append(
            pltpu.make_async_copy(feat_ref.at[rows], own_ref.at[pl.ds(k * BLOCK_ROWS, BLOCK_ROWS)], sems.at[k])
        )
    rows = pl.ds(pl.multiple_of(half * (count // 2), BLOCK_ROWS), count // 2)
    copies.append(pltpu.make_async_copy(feat_ref.at[rows], half_ref, sems.at[4]))
    for copy in copies:
        copy.start()
    scores = jnp.sum(score_ref[...], axis=0, keepdims=True)
    for copy in copies[:4]:
        copy.wait()

    grad = jnp.zeros((1, wide), jnp.float32)
    lane = lax.broadcasted_iota(jnp.int32, (pairs, BLOCK_ROWS), 1)
    sub = lax.broadcasted_iota(jnp.int32, (BLOCK_ROWS, pairs), 0)
    for b in range(blocks):
        cols = slice(b * BLOCK_ROWS, (b + 1) * BLOCK_ROWS)
        select = jnp.where(col_ref[b, :, 0:1] == lane, 1.0, 0.0) - jnp.where(col_ref[b, :, 1:2] == lane, 1.0, 0.0)
        margin = jnp.sum(select * scores[:, cols], axis=1, keepdims=True)
        prob = 1.0 / (1.0 + jnp.exp(-margin))
        weight = prob * (1.0 - prob) * scale
        diffs = lax.dot_general(
            select.astype(jnp.bfloat16), own_ref[:, cols], NT, preferred_element_type=jnp.float32
        )
        diffs = diffs.astype(jnp.bfloat16).astype(jnp.float32)
        weighted = (diffs * weight).astype(jnp.bfloat16)
        grad += jnp.sum(diffs * ((1.0 - prob) * scale), axis=0, keepdims=True)
        back = jnp.where(row_ref[b, 0:1, :] == sub, 1.0, 0.0) - jnp.where(row_ref[b, 1:2, :] == sub, 1.0, 0.0)
        v = jnp.dot(back.astype(jnp.bfloat16), weighted, preferred_element_type=jnp.float32)
        v_high = v.astype(jnp.bfloat16)
        v_ref[cols, 0:wide] = v_high
        v_ref[cols, wide : 2 * wide] = (v - v_high.astype(jnp.float32)).astype(jnp.bfloat16)

    grad_high = grad.astype(jnp.bfloat16).astype(jnp.float32)
    tail_row = lax.broadcasted_iota(jnp.int32, (16, wide), 0)
    tail = jnp.where(tail_row == 0, grad_high, jnp.where(tail_row == 1, grad - grad_high, 0.0))
    tail = tail.astype(jnp.bfloat16)
    copies[4].wait()
    for e in range(0, count // 2 // BLOCK_ROWS, 2):
        part = jnp.dot(
            half_ref[e * BLOCK_ROWS : (e + 2) * BLOCK_ROWS, :], v_ref[...], preferred_element_type=jnp.float32
        )
        part = (part[:, 0:wide] + part[:, wide:]).astype(jnp.bfloat16)
        for zp in range(2):
            d = e // 4 * 4 + zp * 2 + e // 2 % 2
            for k in range(2):
                cols = slice(k * pairs, (k + 1) * pairs)
                out_ref[2 * d + k, 0:BLOCK_ROWS, :] = part[zp * BLOCK_ROWS : (zp + 1) * BLOCK_ROWS, cols]
                out_ref[2 * d + k, BLOCK_ROWS:, :] = tail[:, cols]


def make_gram(at, features, scores, row_pairs, col_pairs, scale, owners):
    count, responses = features.shape
    vmem = pl.BlockSpec(memory_space=pltpu.VMEM)
    return pl.pallas_call(
        functools.partial(gram_kernel, scale),
        in_specs=[
            pl.BlockSpec(memory_space=pltpu.SMEM),
            pl.BlockSpec(memory_space=pl.ANY),
            vmem,
            vmem,
            vmem,
        ],
        out_specs=vmem,
        out_shape=jax.ShapeDtypeStruct((owners, BLOCK_ROWS + 16, 2 * BLOCK_ROWS), jnp.bfloat16),
        scratch_shapes=[
            pltpu.VMEM((4 * BLOCK_ROWS, responses), jnp.bfloat16),
            pltpu.VMEM((count // 2, responses), jnp.bfloat16),
            pltpu.VMEM((responses, 8 * BLOCK_ROWS), jnp.bfloat16),
            pltpu.SemaphoreType.DMA((5,)),
        ],
        compiler_params=pltpu.CompilerParams(vmem_limit_bytes=60 * 1024 * 1024),
        cost_estimate=pl.CostEstimate(
            flops=2 * count * responses * 512, bytes_accessed=count * responses, transcendentals=1024
        ),
    )(at, features, scores, row_pairs, col_pairs)


def swap(value, axis):
    return lax.ppermute(value, axis, [(0, 1), (1, 0)])


def in_order(index, mine, other):
    return jnp.where(index == 0, jnp.stack([mine, other]), jnp.stack([other, mine]))


def per_device(embeddings, landmarks, alpha, pairs):
    rows, pair_count = embeddings.shape[0], pairs.shape[1]
    planes = lax.axis_size(PLANE)
    slabs = lax.axis_size("zh")
    scale = 1.0 / math.sqrt(pair_count * slabs * planes)
    zh, zp = lax.axis_index("zh"), lax.axis_index("zp")

    low, high = embeddings[: rows // 2], embeddings[rows // 2 :]
    kept, sent = jnp.where(zp == 0, low, high), jnp.where(zp == 0, high, low)
    emb = lax.all_gather(in_order(zp, kept, swap(sent, "zp")), RING)
    emb = emb.reshape((-1,) + emb.shape[-2:])

    half = landmarks.shape[0] // slabs
    low, high = landmarks[:half], landmarks[half:]
    kept, sent = jnp.where(zh == 0, low, high), jnp.where(zh == 0, high, low)
    part = in_order(zh, kept, swap(sent, "zh")).transpose(1, 0, 2).reshape(half, -1)
    part = in_order(zp, part, swap(part, "zp")).reshape(2 * half, -1)
    land = lax.all_to_all(jnp.broadcast_to(part[None], (planes,) + part.shape), PLANE, 0, 0, tiled=True)

    own_alpha = jnp.where(zh == 0, alpha[:half], alpha[half:])
    own_alpha = in_order(zp, own_alpha, swap(own_alpha, "zp")).reshape(-1, 1)

    blocks = rows // BLOCK_ROWS
    local = pairs.reshape(2, blocks, -1) - BLOCK_ROWS * jnp.arange(blocks, dtype=pairs.dtype)[None, :, None]
    local = jnp.where(zp == 0, local[:, : blocks // 2], local[:, blocks // 2 :]).transpose(1, 0, 2)
    row_pairs = in_order(zh, local, swap(local, "zh")).reshape(blocks, 2, -1)
    col_pairs = row_pairs.transpose(0, 2, 1)

    mine, score = make_features(emb, land, own_alpha, slabs)
    features = lax.all_gather(mine, RING, axis=0, tiled=True)
    ring = lax.axis_size(RING)
    scores = lax.all_to_all(jnp.broadcast_to(score, (ring, score.shape[1])), RING, 0, 0, tiled=True)
    at = jnp.stack([zh, lax.axis_index(("zm", "c"))]).astype(jnp.int32)
    parts = make_gram(at, features, scores, row_pairs, col_pairs, scale, 2 * planes)
    parts = lax.all_to_all(parts, PLANE + ("zp",), 0, 0, tiled=True)
    total = jnp.sum(parts.astype(jnp.float32), axis=0)
    return total[:BLOCK_ROWS], total[BLOCK_ROWS] + total[BLOCK_ROWS + 1]


def solution(mesh):
    fine = Mesh(mesh.devices.reshape(4, 4, 2, 4, 2, 2), ("y", "x", "zh", "zm", "zp", "c"))
    dp, land = ("y", "x", "zh"), ("zm", "zp", "c")
    return jax.shard_map(
        per_device,
        mesh=fine,
        in_specs=(P(dp, land), P(land, dp), P(land), P(None, dp)),
        out_specs=(P(dp, land), P(land)),
        check_vma=False,
    )
```

```python
import functools
import math

import jax
import jax.numpy as jnp
from jax import lax
from jax.experimental import pallas as pl
from jax.experimental.pallas import tpu as pltpu
from jax.sharding import Mesh, PartitionSpec as P

EMBED_WIDTH = 4096
BLOCK_ROWS = 128
BETA = 0.5 * math.sqrt(EMBED_WIDTH)
RING = ("zh", "zm", "c")
PLANE = ("y", "x")
NT = (((1,), (1,)), ((), ()))


def features_kernel(emb_ref, land_ref, alpha_ref, out_ref, score_ref):
    chunks, rows, width = emb_ref.shape
    count = land_ref.shape[1]
    total = jnp.zeros((rows, count), jnp.float32)
    resp = jnp.zeros((rows, 128), jnp.float32)
    land = jnp.zeros((count, 128), jnp.float32)
    for j in range(chunks):
        zm, c, zp = j // 4, j // 2 % 2, j % 2
        at = zm * 4 + zp * 2 + c
        total += lax.dot_general(emb_ref[j], land_ref[at], NT, preferred_element_type=jnp.float32)
        for lane in range(0, width, 128):
            part = emb_ref[j, :, lane : lane + 128].astype(jnp.float32)
            resp += part * part
            part = land_ref[at, :, lane : lane + 128].astype(jnp.float32)
            land += part * part
    ones = jnp.ones((8, 128), jnp.float32)
    norm = lax.dot_general(ones, land, NT, precision=lax.Precision.HIGHEST, preferred_element_type=jnp.float32)[0:1]
    square = jnp.sum(resp, axis=1, keepdims=True)
    value = BETA * total * lax.rsqrt(square + 1e-06) * lax.rsqrt(norm + 1e-06)
    features = jnp.exp(value).T.astype(out_ref.dtype)
    out_ref[...] = features
    score_ref[...] = jnp.sum(features.astype(jnp.float32) * alpha_ref[...], axis=0, keepdims=True)


def make_features(emb, land, alpha, slabs):
    chunks, rows, part = emb.shape
    count = land.shape[1]
    each = chunks // slabs
    return pl.pallas_call(
        features_kernel,
        grid=(slabs,),
        in_specs=[
            pl.BlockSpec((each, rows, part), lambda s: (s, 0, 0)),
            pl.BlockSpec(land.shape, lambda s: (0, 0, 0)),
            pl.BlockSpec((count, 1), lambda s: (0, 0)),
        ],
        out_specs=[
            pl.BlockSpec((count, rows), lambda s: (0, s)),
            pl.BlockSpec((1, rows), lambda s: (0, s)),
        ],
        out_shape=[
            jax.ShapeDtypeStruct((count, slabs * rows), jnp.bfloat16),
            jax.ShapeDtypeStruct((1, slabs * rows), jnp.float32),
        ],
        compiler_params=pltpu.CompilerParams(vmem_limit_bytes=60 * 1024 * 1024),
        cost_estimate=pl.CostEstimate(
            flops=2 * count * chunks * rows * part,
            bytes_accessed=2 * chunks * rows * part,
            transcendentals=count * slabs * rows,
        ),
    )(emb, land, alpha)


def factor_kernel(scale, own_ref, score_ref, row_ref, col_ref, v_ref, tail_ref):
    wide, responses = own_ref.shape
    pairs = 2 * BLOCK_ROWS
    scores = jnp.sum(score_ref[...], axis=0, keepdims=True)
    grad = jnp.zeros((1, wide), jnp.float32)
    lane = lax.broadcasted_iota(jnp.int32, (pairs, BLOCK_ROWS), 1)
    sub = lax.broadcasted_iota(jnp.int32, (BLOCK_ROWS, pairs), 0)
    for b in range(responses // BLOCK_ROWS):
        cols = slice(b * BLOCK_ROWS, (b + 1) * BLOCK_ROWS)
        select = jnp.where(col_ref[b, :, 0:1] == lane, 1.0, 0.0) - jnp.where(col_ref[b, :, 1:2] == lane, 1.0, 0.0)
        margin = jnp.sum(select * scores[:, cols], axis=1, keepdims=True)
        prob = 1.0 / (1.0 + jnp.exp(-margin))
        weight = prob * (1.0 - prob) * scale
        diffs = lax.dot_general(
            select.astype(jnp.bfloat16), own_ref[:, cols], NT, preferred_element_type=jnp.float32
        )
        diffs = diffs.astype(jnp.bfloat16).astype(jnp.float32)
        weighted = (diffs * weight).astype(jnp.bfloat16)
        grad += jnp.sum(diffs * ((1.0 - prob) * scale), axis=0, keepdims=True)
        back = jnp.where(row_ref[b, 0:1, :] == sub, 1.0, 0.0) - jnp.where(row_ref[b, 1:2, :] == sub, 1.0, 0.0)
        v = jnp.dot(back.astype(jnp.bfloat16), weighted, preferred_element_type=jnp.float32)
        v_high = v.astype(jnp.bfloat16)
        v_ref[cols, 0:wide] = v_high
        v_ref[cols, wide : 2 * wide] = (v - v_high.astype(jnp.float32)).astype(jnp.bfloat16)

    high = grad.astype(jnp.bfloat16).astype(jnp.float32)
    low = grad - high
    row = lax.broadcasted_iota(jnp.int32, (16, BLOCK_ROWS), 0)
    for k in range(2):
        left = slice(2 * k * BLOCK_ROWS, (2 * k + 1) * BLOCK_ROWS)
        right = slice((2 * k + 1) * BLOCK_ROWS, (2 * k + 2) * BLOCK_ROWS)
        tail = jnp.zeros((16, BLOCK_ROWS), jnp.float32)
        for at, value in enumerate((high[:, left], high[:, right], low[:, left], low[:, right])):
            tail = jnp.where(row == at, value, tail)
        tail_ref[k] = tail.astype(jnp.bfloat16)


def make_factor(own, scores, row_pairs, col_pairs, scale):
    wide, responses = own.shape
    vmem = pl.BlockSpec(memory_space=pltpu.VMEM)
    return pl.pallas_call(
        functools.partial(factor_kernel, scale),
        in_specs=[vmem] * 4,
        out_specs=[vmem, vmem],
        out_shape=[
            jax.ShapeDtypeStruct((responses, 2 * wide), jnp.bfloat16),
            jax.ShapeDtypeStruct((2, 16, BLOCK_ROWS), jnp.bfloat16),
        ],
        compiler_params=pltpu.CompilerParams(vmem_limit_bytes=40 * 1024 * 1024),
        cost_estimate=pl.CostEstimate(
            flops=4 * 2 * responses * BLOCK_ROWS * wide, bytes_accessed=6 * wide * responses, transcendentals=1024
        ),
    )(own, scores, row_pairs, col_pairs)


def gram_kernel(at_ref, feat_ref, v_ref, tail_ref, out_ref):
    wide = v_ref.shape[1] // 2
    step = 2 * BLOCK_ROWS
    for c in range(2):
        part = jnp.dot(feat_ref[c * step : (c + 1) * step, :], v_ref[...], preferred_element_type=jnp.float32)
        part = (part[:, 0:wide] + part[:, wide:]).astype(jnp.bfloat16)
        for zp in range(2):
            for k in range(2):
                for side in range(2):
                    at = (2 * k + side) * BLOCK_ROWS
                    out_ref[0, zp, c, k, side * BLOCK_ROWS : (side + 1) * BLOCK_ROWS, :] = part[
                        zp * BLOCK_ROWS : (zp + 1) * BLOCK_ROWS, at : at + BLOCK_ROWS
                    ]
                out_ref[0, zp, c, k, 2 * BLOCK_ROWS :, :] = tail_ref[k]


def make_gram(at, features, factor, tail, owners):
    count, responses = features.shape
    steps = owners // 8
    rows = 2 * BLOCK_ROWS + 16
    part = pl.pallas_call(
        gram_kernel,
        grid_spec=pltpu.PrefetchScalarGridSpec(
            num_scalar_prefetch=1,
            grid=(steps,),
            in_specs=[
                pl.BlockSpec((count // 2 // steps, responses), lambda n, at: (at[0] * steps + n, 0)),
                pl.BlockSpec(factor.shape, lambda n, at: (0, 0)),
                pl.BlockSpec(tail.shape, lambda n, at: (0, 0, 0)),
            ],
            out_specs=pl.BlockSpec((1, 2, 2, 2, rows, BLOCK_ROWS), lambda n, at: (n, 0, 0, 0, 0, 0)),
        ),
        out_shape=jax.ShapeDtypeStruct((steps, 2, 2, 2, rows, BLOCK_ROWS), jnp.bfloat16),
        compiler_params=pltpu.CompilerParams(vmem_limit_bytes=60 * 1024 * 1024),
        cost_estimate=pl.CostEstimate(
            flops=2 * count * responses * 512, bytes_accessed=count * responses, transcendentals=0
        ),
    )(at, features, factor, tail)
    return part.reshape(owners, rows, BLOCK_ROWS)


def swap(value, axis):
    return lax.ppermute(value, axis, [(0, 1), (1, 0)])


def in_order(index, mine, other):
    return jnp.where(index == 0, jnp.stack([mine, other]), jnp.stack([other, mine]))


def per_device(embeddings, landmarks, alpha, pairs):
    rows, pair_count = embeddings.shape[0], pairs.shape[1]
    planes = lax.axis_size(PLANE)
    slabs = lax.axis_size("zh")
    scale = 1.0 / math.sqrt(pair_count * slabs * planes)
    zh, zp = lax.axis_index("zh"), lax.axis_index("zp")

    low, high = embeddings[: rows // 2], embeddings[rows // 2 :]
    kept, sent = jnp.where(zp == 0, low, high), jnp.where(zp == 0, high, low)
    emb = lax.all_gather(in_order(zp, kept, swap(sent, "zp")), RING)
    emb = emb.reshape((-1,) + emb.shape[-2:])

    half = landmarks.shape[0] // slabs
    part = in_order(zh, landmarks, swap(landmarks, "zh")).transpose(1, 0, 2).reshape(slabs * half, -1)
    part = in_order(zp, part, swap(part, "zp"))
    low, high = part[:, :half].reshape(2 * half, -1), part[:, half:].reshape(2 * half, -1)

    def spread(part):
        return lax.all_to_all(jnp.broadcast_to(part[None], (planes,) + part.shape), PLANE, 0, 0, tiled=True)

    land = spread(jnp.where(zh == 0, low, high))

    own_alpha = jnp.where(zh == 0, alpha[:half], alpha[half:])
    own_alpha = in_order(zp, own_alpha, swap(own_alpha, "zp")).reshape(-1, 1)

    blocks = rows // BLOCK_ROWS
    local = pairs.reshape(2, blocks, -1) - BLOCK_ROWS * jnp.arange(blocks, dtype=pairs.dtype)[None, :, None]
    local = jnp.where(zp == 0, local[:, : blocks // 2], local[:, blocks // 2 :]).transpose(1, 0, 2)
    row_pairs = in_order(zh, local, swap(local, "zh")).reshape(blocks, 2, -1)
    col_pairs = row_pairs.transpose(0, 2, 1)

    mine, score = make_features(emb, land, own_alpha, slabs)
    features = lax.all_gather(mine, RING, axis=0, tiled=True)
    ring = lax.axis_size(RING)
    scores = lax.all_to_all(jnp.broadcast_to(score, (ring, score.shape[1])), RING, 0, 0, tiled=True)

    ready = (score[0, 0] == score[0, 0]) | (zh < 0)
    other_land = spread(jnp.where(ready, jnp.where(zh == 0, high, low), jnp.zeros_like(low)))
    other, _ = make_features(emb, other_land, own_alpha, slabs)
    own = in_order(zh, mine.reshape(2, half, -1), other.reshape(2, half, -1))
    own = own.transpose(1, 0, 2, 3).reshape(4 * half, -1)
    factor, tail = make_factor(own, scores, row_pairs, col_pairs, scale)

    at = zh.astype(jnp.int32).reshape(1)
    parts = make_gram(at, features, factor, tail, 2 * planes)
    parts = lax.all_to_all(parts, PLANE + ("zp",), 0, 0, tiled=True)
    total = jnp.sum(parts.astype(jnp.float32), axis=0)
    gram = jnp.concatenate([total[:BLOCK_ROWS], total[BLOCK_ROWS : 2 * BLOCK_ROWS]], axis=1)
    tail = total[2 * BLOCK_ROWS :]
    return gram, jnp.concatenate([tail[0] + tail[2], tail[1] + tail[3]])


def solution(mesh):
    fine = Mesh(mesh.devices.reshape(4, 4, 2, 4, 2, 2), ("y", "x", "zh", "zm", "zp", "c"))
    dp, land = ("y", "x", "zh"), ("zm", "zp", "c")
    return jax.shard_map(
        per_device,
        mesh=fine,
        in_specs=(P(dp, land), P(land, dp), P(land), P(None, dp)),
        out_specs=(P(dp, land), P(land)),
        check_vma=False,
    )
```

```python
import functools
import math

import jax
import jax.numpy as jnp
from jax import lax
from jax.experimental import pallas as pl
from jax.experimental.pallas import tpu as pltpu
from jax.sharding import Mesh, PartitionSpec as P

EMBED_WIDTH = 4096
BLOCK_ROWS = 128
BETA = 0.5 * math.sqrt(EMBED_WIDTH)
RING = ("zh", "zm", "c")
PLANE = ("y", "x")
NT = (((1,), (1,)), ((), ()))


def features_kernel(emb_ref, land_ref, alpha_ref, out_ref, score_ref):
    chunks, rows, width = emb_ref.shape
    count = land_ref.shape[1]
    total = jnp.zeros((rows, count), jnp.float32)
    resp = jnp.zeros((rows, 128), jnp.float32)
    land = jnp.zeros((count, 128), jnp.float32)
    for j in range(chunks):
        zm, c, zp = j // 4, j // 2 % 2, j % 2
        at = zm * 4 + zp * 2 + c
        total += lax.dot_general(emb_ref[j], land_ref[at], NT, preferred_element_type=jnp.float32)
        for lane in range(0, width, 128):
            part = emb_ref[j, :, lane : lane + 128].astype(jnp.float32)
            resp += part * part
            part = land_ref[at, :, lane : lane + 128].astype(jnp.float32)
            land += part * part
    ones = jnp.ones((8, 128), jnp.float32)
    norm = lax.dot_general(ones, land, NT, precision=lax.Precision.HIGHEST, preferred_element_type=jnp.float32)[0:1]
    square = jnp.sum(resp, axis=1, keepdims=True)
    value = BETA * total * lax.rsqrt(square + 1e-06) * lax.rsqrt(norm + 1e-06)
    features = jnp.exp(value).T.astype(out_ref.dtype)
    out_ref[...] = features
    score_ref[...] = jnp.sum(features.astype(jnp.float32) * alpha_ref[...], axis=0, keepdims=True)


def make_features(emb, land, alpha, slabs):
    chunks, rows, part = emb.shape
    count = land.shape[1]
    each = chunks // slabs
    return pl.pallas_call(
        features_kernel,
        grid=(slabs,),
        in_specs=[
            pl.BlockSpec((each, rows, part), lambda s: (s, 0, 0)),
            pl.BlockSpec(land.shape, lambda s: (0, 0, 0)),
            pl.BlockSpec((count, 1), lambda s: (0, 0)),
        ],
        out_specs=[
            pl.BlockSpec((count, rows), lambda s: (0, s)),
            pl.BlockSpec((1, rows), lambda s: (0, s)),
        ],
        out_shape=[
            jax.ShapeDtypeStruct((count, slabs * rows), jnp.bfloat16),
            jax.ShapeDtypeStruct((1, slabs * rows), jnp.float32),
        ],
        compiler_params=pltpu.CompilerParams(vmem_limit_bytes=60 * 1024 * 1024),
        cost_estimate=pl.CostEstimate(
            flops=2 * count * chunks * rows * part,
            bytes_accessed=2 * chunks * rows * part,
            transcendentals=count * slabs * rows,
        ),
    )(emb, land, alpha)


def gram_kernel(scale, at_ref, feat_ref, score_ref, row_ref, col_ref, out_ref, own_ref, half_ref, v_ref, sems):
    half, own = at_ref[0], at_ref[1]
    count, responses = feat_ref.shape
    blocks = responses // BLOCK_ROWS
    pairs = 2 * BLOCK_ROWS
    wide = 4 * BLOCK_ROWS
    copies = []
    for k in range(4):
        zp, zh = k // 2, k % 2
        rows = pl.ds(
            pl.multiple_of(zh * (count // 2) + own * pairs + zp * BLOCK_ROWS, BLOCK_ROWS), BLOCK_ROWS
        )
        copies.append(
            pltpu.make_async_copy(feat_ref.at[rows], own_ref.at[pl.ds(k * BLOCK_ROWS, BLOCK_ROWS)], sems.at[k])
        )
    rows = pl.ds(pl.multiple_of(half * (count // 2), BLOCK_ROWS), count // 2)
    copies.append(pltpu.make_async_copy(feat_ref.at[rows], half_ref, sems.at[4]))
    for copy in copies:
        copy.start()
    scores = jnp.sum(score_ref[...], axis=0, keepdims=True)
    for copy in copies[:4]:
        copy.wait()

    grad = jnp.zeros((1, wide), jnp.float32)
    lane = lax.broadcasted_iota(jnp.int32, (pairs, BLOCK_ROWS), 1)
    sub = lax.broadcasted_iota(jnp.int32, (BLOCK_ROWS, pairs), 0)
    for b in range(blocks):
        cols = slice(b * BLOCK_ROWS, (b + 1) * BLOCK_ROWS)
        select = jnp.where(col_ref[b, :, 0:1] == lane, 1.0, 0.0) - jnp.where(col_ref[b, :, 1:2] == lane, 1.0, 0.0)
        margin = jnp.sum(select * scores[:, cols], axis=1, keepdims=True)
        prob = 1.0 / (1.0 + jnp.exp(-margin))
        weight = prob * (1.0 - prob) * scale
        diffs = lax.dot_general(
            select.astype(jnp.bfloat16), own_ref[:, cols], NT, preferred_element_type=jnp.float32
        )
        diffs = diffs.astype(jnp.bfloat16).astype(jnp.float32)
        weighted = (diffs * weight).astype(jnp.bfloat16)
        grad += jnp.sum(diffs * ((1.0 - prob) * scale), axis=0, keepdims=True)
        back = jnp.where(row_ref[b, 0:1, :] == sub, 1.0, 0.0) - jnp.where(row_ref[b, 1:2, :] == sub, 1.0, 0.0)
        v = jnp.dot(back.astype(jnp.bfloat16), weighted, preferred_element_type=jnp.float32)
        v_high = v.astype(jnp.bfloat16)
        v_ref[cols, 0:wide] = v_high
        v_ref[cols, wide : 2 * wide] = (v - v_high.astype(jnp.float32)).astype(jnp.bfloat16)

    high = grad.astype(jnp.bfloat16).astype(jnp.float32)
    low = grad - high
    row = lax.broadcasted_iota(jnp.int32, (16, BLOCK_ROWS), 0)
    tails = []
    for k in range(2):
        left = slice(2 * k * BLOCK_ROWS, (2 * k + 1) * BLOCK_ROWS)
        right = slice((2 * k + 1) * BLOCK_ROWS, (2 * k + 2) * BLOCK_ROWS)
        tail = jnp.zeros((16, BLOCK_ROWS), jnp.float32)
        for at, value in enumerate((high[:, left], high[:, right], low[:, left], low[:, right])):
            tail = jnp.where(row == at, value, tail)
        tails.append(tail.astype(jnp.bfloat16))
    copies[4].wait()
    for e in range(0, count // 2 // BLOCK_ROWS, 2):
        part = jnp.dot(
            half_ref[e * BLOCK_ROWS : (e + 2) * BLOCK_ROWS, :], v_ref[...], preferred_element_type=jnp.float32
        )
        part = (part[:, 0:wide] + part[:, wide:]).astype(jnp.bfloat16)
        for zp in range(2):
            d = e // 4 * 4 + zp * 2 + e // 2 % 2
            for k in range(2):
                for side in range(2):
                    at = (2 * k + side) * BLOCK_ROWS
                    out_ref[2 * d + k, side * BLOCK_ROWS : (side + 1) * BLOCK_ROWS, :] = part[
                        zp * BLOCK_ROWS : (zp + 1) * BLOCK_ROWS, at : at + BLOCK_ROWS
                    ]
                out_ref[2 * d + k, 2 * BLOCK_ROWS :, :] = tails[k]


def make_gram(at, features, scores, row_pairs, col_pairs, scale, owners):
    count, responses = features.shape
    vmem = pl.BlockSpec(memory_space=pltpu.VMEM)
    return pl.pallas_call(
        functools.partial(gram_kernel, scale),
        in_specs=[
            pl.BlockSpec(memory_space=pltpu.SMEM),
            pl.BlockSpec(memory_space=pl.ANY),
            vmem,
            vmem,
            vmem,
        ],
        out_specs=vmem,
        out_shape=jax.ShapeDtypeStruct((owners, 2 * BLOCK_ROWS + 16, BLOCK_ROWS), jnp.bfloat16),
        scratch_shapes=[
            pltpu.VMEM((4 * BLOCK_ROWS, responses), jnp.bfloat16),
            pltpu.VMEM((count // 2, responses), jnp.bfloat16),
            pltpu.VMEM((responses, 8 * BLOCK_ROWS), jnp.bfloat16),
            pltpu.SemaphoreType.DMA((5,)),
        ],
        compiler_params=pltpu.CompilerParams(vmem_limit_bytes=60 * 1024 * 1024),
        cost_estimate=pl.CostEstimate(
            flops=2 * count * responses * 512, bytes_accessed=count * responses, transcendentals=1024
        ),
    )(at, features, scores, row_pairs, col_pairs)


def swap(value, axis):
    return lax.ppermute(value, axis, [(0, 1), (1, 0)])


def in_order(index, mine, other):
    return jnp.where(index == 0, jnp.stack([mine, other]), jnp.stack([other, mine]))


def per_device(embeddings, landmarks, alpha, pairs):
    rows, pair_count = embeddings.shape[0], pairs.shape[1]
    planes = lax.axis_size(PLANE)
    slabs = lax.axis_size("zh")
    scale = 1.0 / math.sqrt(pair_count * slabs * planes)
    zh, zp = lax.axis_index("zh"), lax.axis_index("zp")

    low, high = embeddings[: rows // 2], embeddings[rows // 2 :]
    kept, sent = jnp.where(zp == 0, low, high), jnp.where(zp == 0, high, low)
    emb = lax.all_gather(in_order(zp, kept, swap(sent, "zp")), RING)
    emb = emb.reshape((-1,) + emb.shape[-2:])

    half = landmarks.shape[0] // slabs
    low, high = landmarks[:half], landmarks[half:]
    kept, sent = jnp.where(zh == 0, low, high), jnp.where(zh == 0, high, low)
    part = in_order(zh, kept, swap(sent, "zh")).transpose(1, 0, 2).reshape(half, -1)
    part = in_order(zp, part, swap(part, "zp")).reshape(2 * half, -1)
    land = lax.all_to_all(jnp.broadcast_to(part[None], (planes,) + part.shape), PLANE, 0, 0, tiled=True)

    own_alpha = jnp.where(zh == 0, alpha[:half], alpha[half:])
    own_alpha = in_order(zp, own_alpha, swap(own_alpha, "zp")).reshape(-1, 1)

    blocks = rows // BLOCK_ROWS
    local = pairs.reshape(2, blocks, -1) - BLOCK_ROWS * jnp.arange(blocks, dtype=pairs.dtype)[None, :, None]
    local = jnp.where(zp == 0, local[:, : blocks // 2], local[:, blocks // 2 :]).transpose(1, 0, 2)
    row_pairs = in_order(zh, local, swap(local, "zh")).reshape(blocks, 2, -1)
    col_pairs = row_pairs.transpose(0, 2, 1)

    mine, score = make_features(emb, land, own_alpha, slabs)
    features = lax.all_gather(mine, RING, axis=0, tiled=True)
    ring = lax.axis_size(RING)
    scores = lax.all_to_all(jnp.broadcast_to(score, (ring, score.shape[1])), RING, 0, 0, tiled=True)
    at = jnp.stack([zh, lax.axis_index(("zm", "c"))]).astype(jnp.int32)
    parts = make_gram(at, features, scores, row_pairs, col_pairs, scale, 2 * planes)
    parts = lax.all_to_all(parts, PLANE + ("zp",), 0, 0, tiled=True)
    total = jnp.sum(parts.astype(jnp.float32), axis=0)
    gram = jnp.concatenate([total[:BLOCK_ROWS], total[BLOCK_ROWS : 2 * BLOCK_ROWS]], axis=1)
    tail = total[2 * BLOCK_ROWS :]
    return gram, jnp.concatenate([tail[0] + tail[2], tail[1] + tail[3]])


def solution(mesh):
    fine = Mesh(mesh.devices.reshape(4, 4, 2, 4, 2, 2), ("y", "x", "zh", "zm", "zp", "c"))
    dp, land = ("y", "x", "zh"), ("zm", "zp", "c")
    return jax.shard_map(
        per_device,
        mesh=fine,
        in_specs=(P(dp, land), P(land, dp), P(land), P(None, dp)),
        out_specs=(P(dp, land), P(land)),
        check_vma=False,
    )
```

```python
import functools
import math

import jax
import jax.numpy as jnp
from jax import lax
from jax.experimental import pallas as pl
from jax.experimental.pallas import tpu as pltpu
from jax.sharding import Mesh, PartitionSpec as P

EMBED_WIDTH = 4096
BLOCK_ROWS = 128
BETA = 0.5 * math.sqrt(EMBED_WIDTH)
RING = ("zh", "zm", "c")
PLANE = ("y", "x")
NT = (((1,), (1,)), ((), ()))


def norms_kernel(land_ref, out_ref):
    chunks, count, width = land_ref.shape
    total = jnp.zeros((count, 128), jnp.float32)
    for j in range(chunks):
        for lane in range(0, width, 128):
            part = land_ref[j, :, lane : lane + 128].astype(jnp.float32)
            total += part * part
    ones = jnp.ones((8, 128), jnp.float32)
    norm = lax.dot_general(ones, total, NT, precision=lax.Precision.HIGHEST, preferred_element_type=jnp.float32)
    out_ref[...] = lax.rsqrt(norm[0:1] + 1e-06)


def make_norms(land):
    return pl.pallas_call(
        norms_kernel,
        in_specs=[pl.BlockSpec(memory_space=pltpu.VMEM)],
        out_specs=pl.BlockSpec(memory_space=pltpu.VMEM),
        out_shape=jax.ShapeDtypeStruct((1, land.shape[1]), jnp.float32),
        compiler_params=pltpu.CompilerParams(vmem_limit_bytes=16 * 1024 * 1024),
        cost_estimate=pl.CostEstimate(flops=2 * land.size, bytes_accessed=2 * land.size, transcendentals=256),
    )(land)


def features_kernel(emb_ref, land_ref, norm_ref, alpha_ref, out_ref, score_ref):
    chunks, rows, width = emb_ref.shape
    count = land_ref.shape[1]
    total = jnp.zeros((rows, count), jnp.float32)
    resp = jnp.zeros((rows, 128), jnp.float32)
    for j in range(chunks):
        zm, c, zp = j // 4, j // 2 % 2, j % 2
        at = zm * 4 + zp * 2 + c
        total += lax.dot_general(emb_ref[j], land_ref[at], NT, preferred_element_type=jnp.float32)
        for lane in range(0, width, 128):
            part = emb_ref[j, :, lane : lane + 128].astype(jnp.float32)
            resp += part * part
    square = jnp.sum(resp, axis=1, keepdims=True)
    value = BETA * total * lax.rsqrt(square + 1e-06) * norm_ref[...]
    features = jnp.exp(value).T.astype(out_ref.dtype)
    out_ref[...] = features
    score_ref[...] = jnp.sum(features.astype(jnp.float32) * alpha_ref[...], axis=0, keepdims=True)


def make_features(emb, land, norms, alpha, slabs):
    chunks, rows, part = emb.shape
    count = land.shape[1]
    each = chunks // slabs
    return pl.pallas_call(
        features_kernel,
        grid=(slabs,),
        in_specs=[
            pl.BlockSpec((each, rows, part), lambda s: (s, 0, 0)),
            pl.BlockSpec(land.shape, lambda s: (0, 0, 0)),
            pl.BlockSpec((1, count), lambda s: (0, 0)),
            pl.BlockSpec((count, 1), lambda s: (0, 0)),
        ],
        out_specs=[
            pl.BlockSpec((count, rows), lambda s: (0, s)),
            pl.BlockSpec((1, rows), lambda s: (0, s)),
        ],
        out_shape=[
            jax.ShapeDtypeStruct((count, slabs * rows), jnp.bfloat16),
            jax.ShapeDtypeStruct((1, slabs * rows), jnp.float32),
        ],
        compiler_params=pltpu.CompilerParams(vmem_limit_bytes=60 * 1024 * 1024),
        cost_estimate=pl.CostEstimate(
            flops=2 * count * chunks * rows * part,
            bytes_accessed=2 * chunks * rows * part,
            transcendentals=count * slabs * rows,
        ),
    )(emb, land, norms, alpha)


def gram_kernel(scale, at_ref, feat_ref, score_ref, row_ref, col_ref, out_ref, own_ref, half_ref, v_ref, sems):
    half, own = at_ref[0], at_ref[1]
    count, responses = feat_ref.shape
    blocks = responses // BLOCK_ROWS
    pairs = 2 * BLOCK_ROWS
    wide = 4 * BLOCK_ROWS
    copies = []
    for k in range(4):
        zp, zh = k // 2, k % 2
        rows = pl.ds(
            pl.multiple_of(zh * (count // 2) + own * pairs + zp * BLOCK_ROWS, BLOCK_ROWS), BLOCK_ROWS
        )
        copies.append(
            pltpu.make_async_copy(feat_ref.at[rows], own_ref.at[pl.ds(k * BLOCK_ROWS, BLOCK_ROWS)], sems.at[k])
        )
    rows = pl.ds(pl.multiple_of(half * (count // 2), BLOCK_ROWS), count // 2)
    copies.append(pltpu.make_async_copy(feat_ref.at[rows], half_ref, sems.at[4]))
    for copy in copies:
        copy.start()
    scores = jnp.sum(score_ref[...], axis=0, keepdims=True)
    for copy in copies[:4]:
        copy.wait()

    grad = jnp.zeros((1, wide), jnp.float32)
    lane = lax.broadcasted_iota(jnp.int32, (pairs, BLOCK_ROWS), 1)
    sub = lax.broadcasted_iota(jnp.int32, (BLOCK_ROWS, pairs), 0)
    for b in range(blocks):
        cols = slice(b * BLOCK_ROWS, (b + 1) * BLOCK_ROWS)
        select = jnp.where(col_ref[b, :, 0:1] == lane, 1.0, 0.0) - jnp.where(col_ref[b, :, 1:2] == lane, 1.0, 0.0)
        margin = jnp.sum(select * scores[:, cols], axis=1, keepdims=True)
        prob = 1.0 / (1.0 + jnp.exp(-margin))
        weight = prob * (1.0 - prob) * scale
        diffs = lax.dot_general(
            select.astype(jnp.bfloat16), own_ref[:, cols], NT, preferred_element_type=jnp.float32
        )
        diffs = diffs.astype(jnp.bfloat16).astype(jnp.float32)
        weighted = (diffs * weight).astype(jnp.bfloat16)
        grad += jnp.sum(diffs * ((1.0 - prob) * scale), axis=0, keepdims=True)
        back = jnp.where(row_ref[b, 0:1, :] == sub, 1.0, 0.0) - jnp.where(row_ref[b, 1:2, :] == sub, 1.0, 0.0)
        v = jnp.dot(back.astype(jnp.bfloat16), weighted, preferred_element_type=jnp.float32)
        v_high = v.astype(jnp.bfloat16)
        v_ref[cols, 0:wide] = v_high
        v_ref[cols, wide : 2 * wide] = (v - v_high.astype(jnp.float32)).astype(jnp.bfloat16)

    high = grad.astype(jnp.bfloat16).astype(jnp.float32)
    low = grad - high
    row = lax.broadcasted_iota(jnp.int32, (16, BLOCK_ROWS), 0)
    tails = []
    for k in range(2):
        left = slice(2 * k * BLOCK_ROWS, (2 * k + 1) * BLOCK_ROWS)
        right = slice((2 * k + 1) * BLOCK_ROWS, (2 * k + 2) * BLOCK_ROWS)
        tail = jnp.zeros((16, BLOCK_ROWS), jnp.float32)
        for at, value in enumerate((high[:, left], high[:, right], low[:, left], low[:, right])):
            tail = jnp.where(row == at, value, tail)
        tails.append(tail.astype(jnp.bfloat16))
    copies[4].wait()
    for e in range(0, count // 2 // BLOCK_ROWS, 2):
        part = jnp.dot(
            half_ref[e * BLOCK_ROWS : (e + 2) * BLOCK_ROWS, :], v_ref[...], preferred_element_type=jnp.float32
        )
        part = (part[:, 0:wide] + part[:, wide:]).astype(jnp.bfloat16)
        for zp in range(2):
            d = e // 4 * 4 + zp * 2 + e // 2 % 2
            for k in range(2):
                for side in range(2):
                    at = (2 * k + side) * BLOCK_ROWS
                    out_ref[2 * d + k, side * BLOCK_ROWS : (side + 1) * BLOCK_ROWS, :] = part[
                        zp * BLOCK_ROWS : (zp + 1) * BLOCK_ROWS, at : at + BLOCK_ROWS
                    ]
                out_ref[2 * d + k, 2 * BLOCK_ROWS :, :] = tails[k]


def make_gram(at, features, scores, row_pairs, col_pairs, scale, owners):
    count, responses = features.shape
    vmem = pl.BlockSpec(memory_space=pltpu.VMEM)
    return pl.pallas_call(
        functools.partial(gram_kernel, scale),
        in_specs=[
            pl.BlockSpec(memory_space=pltpu.SMEM),
            pl.BlockSpec(memory_space=pl.ANY),
            vmem,
            vmem,
            vmem,
        ],
        out_specs=vmem,
        out_shape=jax.ShapeDtypeStruct((owners, 2 * BLOCK_ROWS + 16, BLOCK_ROWS), jnp.bfloat16),
        scratch_shapes=[
            pltpu.VMEM((4 * BLOCK_ROWS, responses), jnp.bfloat16),
            pltpu.VMEM((count // 2, responses), jnp.bfloat16),
            pltpu.VMEM((responses, 8 * BLOCK_ROWS), jnp.bfloat16),
            pltpu.SemaphoreType.DMA((5,)),
        ],
        compiler_params=pltpu.CompilerParams(vmem_limit_bytes=50 * 1024 * 1024),
        cost_estimate=pl.CostEstimate(
            flops=2 * count * responses * 512, bytes_accessed=count * responses, transcendentals=1024
        ),
    )(at, features, scores, row_pairs, col_pairs)


def swap(value, axis):
    return lax.ppermute(value, axis, [(0, 1), (1, 0)])


def in_order(index, mine, other):
    return jnp.where(index == 0, jnp.stack([mine, other]), jnp.stack([other, mine]))


def per_device(embeddings, landmarks, alpha, pairs):
    rows, pair_count = embeddings.shape[0], pairs.shape[1]
    planes = lax.axis_size(PLANE)
    slabs = lax.axis_size("zh")
    scale = 1.0 / math.sqrt(pair_count * slabs * planes)
    zh, zp = lax.axis_index("zh"), lax.axis_index("zp")

    low, high = embeddings[: rows // 2], embeddings[rows // 2 :]
    kept, sent = jnp.where(zp == 0, low, high), jnp.where(zp == 0, high, low)
    emb = lax.all_gather(in_order(zp, kept, swap(sent, "zp")), RING)
    emb = emb.reshape((-1,) + emb.shape[-2:])

    half = landmarks.shape[0] // slabs
    low, high = landmarks[:half], landmarks[half:]
    kept, sent = jnp.where(zh == 0, low, high), jnp.where(zh == 0, high, low)
    part = in_order(zh, kept, swap(sent, "zh")).transpose(1, 0, 2).reshape(half, -1)
    part = in_order(zp, part, swap(part, "zp")).reshape(2 * half, -1)
    land = lax.all_to_all(jnp.broadcast_to(part[None], (planes,) + part.shape), PLANE, 0, 0, tiled=True)

    own_alpha = jnp.where(zh == 0, alpha[:half], alpha[half:])
    own_alpha = in_order(zp, own_alpha, swap(own_alpha, "zp")).reshape(-1, 1)

    blocks = rows // BLOCK_ROWS
    local = pairs.reshape(2, blocks, -1) - BLOCK_ROWS * jnp.arange(blocks, dtype=pairs.dtype)[None, :, None]
    local = jnp.where(zp == 0, local[:, : blocks // 2], local[:, blocks // 2 :]).transpose(1, 0, 2)
    row_pairs = in_order(zh, local, swap(local, "zh")).reshape(blocks, 2, -1)
    col_pairs = row_pairs.transpose(0, 2, 1)

    mine, score = make_features(emb, land, make_norms(land), own_alpha, slabs)
    features = lax.all_gather(mine, RING, axis=0, tiled=True)
    ring = lax.axis_size(RING)
    scores = lax.all_to_all(jnp.broadcast_to(score, (ring, score.shape[1])), RING, 0, 0, tiled=True)
    at = jnp.stack([zh, lax.axis_index(("zm", "c"))]).astype(jnp.int32)
    parts = make_gram(at, features, scores, row_pairs, col_pairs, scale, 2 * planes)
    parts = lax.all_to_all(parts, PLANE + ("zp",), 0, 0, tiled=True)
    total = jnp.sum(parts.astype(jnp.float32), axis=0)
    gram = jnp.concatenate([total[:BLOCK_ROWS], total[BLOCK_ROWS : 2 * BLOCK_ROWS]], axis=1)
    tail = total[2 * BLOCK_ROWS :]
    return gram, jnp.concatenate([tail[0] + tail[2], tail[1] + tail[3]])


def solution(mesh):
    fine = Mesh(mesh.devices.reshape(4, 4, 2, 4, 2, 2), ("y", "x", "zh", "zm", "zp", "c"))
    dp, land = ("y", "x", "zh"), ("zm", "zp", "c")
    return jax.shard_map(
        per_device,
        mesh=fine,
        in_specs=(P(dp, land), P(land, dp), P(land), P(None, dp)),
        out_specs=(P(dp, land), P(land)),
        check_vma=False,
    )
```

```python
import functools
import math

import jax
import jax.numpy as jnp
from jax import lax
from jax.experimental import pallas as pl
from jax.experimental.pallas import tpu as pltpu
from jax.sharding import Mesh, PartitionSpec as P

EMBED_WIDTH = 4096
BLOCK_ROWS = 128
BETA = 0.5 * math.sqrt(EMBED_WIDTH)
RING = ("zh", "zm", "c")
PLANE = ("y", "x")
NT = (((1,), (1,)), ((), ()))


def norms_kernel(land_ref, out_ref):
    chunks, count, width = land_ref.shape
    total = jnp.zeros((count, 128), jnp.float32)
    for j in range(chunks):
        for lane in range(0, width, 128):
            part = land_ref[j, :, lane : lane + 128].astype(jnp.float32)
            total += part * part
    ones = jnp.ones((8, 128), jnp.float32)
    norm = lax.dot_general(ones, total, NT, precision=lax.Precision.HIGHEST, preferred_element_type=jnp.float32)
    out_ref[...] = lax.rsqrt(norm[0:1] + 1e-06)


def make_norms(land):
    return pl.pallas_call(
        norms_kernel,
        in_specs=[pl.BlockSpec(memory_space=pltpu.VMEM)],
        out_specs=pl.BlockSpec(memory_space=pltpu.VMEM),
        out_shape=jax.ShapeDtypeStruct((1, land.shape[1]), jnp.float32),
        compiler_params=pltpu.CompilerParams(vmem_limit_bytes=16 * 1024 * 1024),
        cost_estimate=pl.CostEstimate(flops=2 * land.size, bytes_accessed=2 * land.size, transcendentals=256),
    )(land)


def features_kernel(emb_ref, land_ref, norm_ref, alpha_ref, out_ref, score_ref):
    chunks, rows, width = emb_ref.shape
    count = land_ref.shape[1]
    total = jnp.zeros((rows, count), jnp.float32)
    resp = jnp.zeros((rows, 128), jnp.float32)
    for j in range(chunks):
        zm, c, zp = j // 4, j // 2 % 2, j % 2
        at = zm * 4 + zp * 2 + c
        total += lax.dot_general(emb_ref[j], land_ref[at], NT, preferred_element_type=jnp.float32)
        for lane in range(0, width, 128):
            part = emb_ref[j, :, lane : lane + 128].astype(jnp.float32)
            resp += part * part
    square = jnp.sum(resp, axis=1, keepdims=True)
    value = BETA * total * lax.rsqrt(square + 1e-06) * norm_ref[...]
    features = jnp.exp(value).T.astype(out_ref.dtype)
    out_ref[...] = features
    score_ref[...] = jnp.sum(features.astype(jnp.float32) * alpha_ref[...], axis=0, keepdims=True)


def make_features(emb, land, norms, alpha, slabs):
    chunks, rows, part = emb.shape
    count = land.shape[1]
    each = chunks // slabs
    return pl.pallas_call(
        features_kernel,
        grid=(slabs,),
        in_specs=[
            pl.BlockSpec((each, rows, part), lambda s: (s, 0, 0)),
            pl.BlockSpec(land.shape, lambda s: (0, 0, 0)),
            pl.BlockSpec((1, count), lambda s: (0, 0)),
            pl.BlockSpec((count, 1), lambda s: (0, 0)),
        ],
        out_specs=[
            pl.BlockSpec((count, rows), lambda s: (0, s)),
            pl.BlockSpec((1, rows), lambda s: (0, s)),
        ],
        out_shape=[
            jax.ShapeDtypeStruct((count, slabs * rows), jnp.bfloat16),
            jax.ShapeDtypeStruct((1, slabs * rows), jnp.float32),
        ],
        compiler_params=pltpu.CompilerParams(vmem_limit_bytes=60 * 1024 * 1024),
        cost_estimate=pl.CostEstimate(
            flops=2 * count * chunks * rows * part,
            bytes_accessed=2 * chunks * rows * part,
            transcendentals=count * slabs * rows,
        ),
    )(emb, land, norms, alpha)


def pairs_kernel(scale, score_ref, row_ref, col_ref, select_ref, back_ref, weight_ref, rest_ref):
    pairs = 2 * BLOCK_ROWS
    scores = jnp.sum(score_ref[...], axis=0, keepdims=True)
    lane = lax.broadcasted_iota(jnp.int32, (pairs, BLOCK_ROWS), 1)
    sub = lax.broadcasted_iota(jnp.int32, (BLOCK_ROWS, pairs), 0)
    for b in range(col_ref.shape[0]):
        cols = slice(b * BLOCK_ROWS, (b + 1) * BLOCK_ROWS)
        select = jnp.where(col_ref[b, :, 0:1] == lane, 1.0, 0.0) - jnp.where(col_ref[b, :, 1:2] == lane, 1.0, 0.0)
        margin = jnp.sum(select * scores[:, cols], axis=1, keepdims=True)
        prob = 1.0 / (1.0 + jnp.exp(-margin))
        weight_ref[b] = prob * (1.0 - prob) * scale
        rest_ref[b] = (1.0 - prob) * scale
        select_ref[b] = select.astype(jnp.bfloat16)
        back = jnp.where(row_ref[b, 0:1, :] == sub, 1.0, 0.0) - jnp.where(row_ref[b, 1:2, :] == sub, 1.0, 0.0)
        back_ref[b] = back.astype(jnp.bfloat16)


def make_pairs(scores, row_pairs, col_pairs, scale):
    blocks, _, pairs = row_pairs.shape
    vmem = pl.BlockSpec(memory_space=pltpu.VMEM)
    return pl.pallas_call(
        functools.partial(pairs_kernel, scale),
        in_specs=[vmem] * 3,
        out_specs=[vmem] * 4,
        out_shape=[
            jax.ShapeDtypeStruct((blocks, pairs, BLOCK_ROWS), jnp.bfloat16),
            jax.ShapeDtypeStruct((blocks, BLOCK_ROWS, pairs), jnp.bfloat16),
            jax.ShapeDtypeStruct((blocks, pairs, 1), jnp.float32),
            jax.ShapeDtypeStruct((blocks, pairs, 1), jnp.float32),
        ],
        compiler_params=pltpu.CompilerParams(vmem_limit_bytes=16 * 1024 * 1024),
        cost_estimate=pl.CostEstimate(flops=1000000, bytes_accessed=2000000, transcendentals=1024),
    )(scores, row_pairs, col_pairs)


def gram_kernel(
    at_ref, feat_ref, select_ref, back_ref, weight_ref, rest_ref, out_ref, own_ref, half_ref, v_ref, sems
):
    half, own = at_ref[0], at_ref[1]
    count, responses = feat_ref.shape
    blocks = responses // BLOCK_ROWS
    pairs = 2 * BLOCK_ROWS
    wide = 4 * BLOCK_ROWS
    copies = []
    for k in range(4):
        zp, zh = k // 2, k % 2
        rows = pl.ds(
            pl.multiple_of(zh * (count // 2) + own * pairs + zp * BLOCK_ROWS, BLOCK_ROWS), BLOCK_ROWS
        )
        copies.append(
            pltpu.make_async_copy(feat_ref.at[rows], own_ref.at[pl.ds(k * BLOCK_ROWS, BLOCK_ROWS)], sems.at[k])
        )
    rows = pl.ds(pl.multiple_of(half * (count // 2), BLOCK_ROWS), count // 2)
    copies.append(pltpu.make_async_copy(feat_ref.at[rows], half_ref, sems.at[4]))
    for copy in copies:
        copy.start()
    for copy in copies[:4]:
        copy.wait()

    grad = jnp.zeros((1, wide), jnp.float32)
    for b in range(blocks):
        cols = slice(b * BLOCK_ROWS, (b + 1) * BLOCK_ROWS)
        diffs = lax.dot_general(select_ref[b], own_ref[:, cols], NT, preferred_element_type=jnp.float32)
        diffs = diffs.astype(jnp.bfloat16).astype(jnp.float32)
        weighted = (diffs * weight_ref[b]).astype(jnp.bfloat16)
        grad += jnp.sum(diffs * rest_ref[b], axis=0, keepdims=True)
        v = jnp.dot(back_ref[b], weighted, preferred_element_type=jnp.float32)
        v_high = v.astype(jnp.bfloat16)
        v_ref[cols, 0:wide] = v_high
        v_ref[cols, wide : 2 * wide] = (v - v_high.astype(jnp.float32)).astype(jnp.bfloat16)

    high = grad.astype(jnp.bfloat16).astype(jnp.float32)
    low = grad - high
    row = lax.broadcasted_iota(jnp.int32, (16, BLOCK_ROWS), 0)
    tails = []
    for k in range(2):
        left = slice(2 * k * BLOCK_ROWS, (2 * k + 1) * BLOCK_ROWS)
        right = slice((2 * k + 1) * BLOCK_ROWS, (2 * k + 2) * BLOCK_ROWS)
        tail = jnp.zeros((16, BLOCK_ROWS), jnp.float32)
        for at, value in enumerate((high[:, left], high[:, right], low[:, left], low[:, right])):
            tail = jnp.where(row == at, value, tail)
        tails.append(tail.astype(jnp.bfloat16))
    copies[4].wait()
    for e in range(0, count // 2 // BLOCK_ROWS, 2):
        part = jnp.dot(
            half_ref[e * BLOCK_ROWS : (e + 2) * BLOCK_ROWS, :], v_ref[...], preferred_element_type=jnp.float32
        )
        part = (part[:, 0:wide] + part[:, wide:]).astype(jnp.bfloat16)
        for zp in range(2):
            d = e // 4 * 4 + zp * 2 + e // 2 % 2
            for k in range(2):
                for side in range(2):
                    at = (2 * k + side) * BLOCK_ROWS
                    out_ref[2 * d + k, side * BLOCK_ROWS : (side + 1) * BLOCK_ROWS, :] = part[
                        zp * BLOCK_ROWS : (zp + 1) * BLOCK_ROWS, at : at + BLOCK_ROWS
                    ]
                out_ref[2 * d + k, 2 * BLOCK_ROWS :, :] = tails[k]


def make_gram(at, features, chosen, owners):
    count, responses = features.shape
    vmem = pl.BlockSpec(memory_space=pltpu.VMEM)
    return pl.pallas_call(
        gram_kernel,
        in_specs=[
            pl.BlockSpec(memory_space=pltpu.SMEM),
            pl.BlockSpec(memory_space=pl.ANY),
            vmem,
            vmem,
            vmem,
            vmem,
        ],
        out_specs=vmem,
        out_shape=jax.ShapeDtypeStruct((owners, 2 * BLOCK_ROWS + 16, BLOCK_ROWS), jnp.bfloat16),
        scratch_shapes=[
            pltpu.VMEM((4 * BLOCK_ROWS, responses), jnp.bfloat16),
            pltpu.VMEM((count // 2, responses), jnp.bfloat16),
            pltpu.VMEM((responses, 8 * BLOCK_ROWS), jnp.bfloat16),
            pltpu.SemaphoreType.DMA((5,)),
        ],
        compiler_params=pltpu.CompilerParams(vmem_limit_bytes=50 * 1024 * 1024),
        cost_estimate=pl.CostEstimate(
            flops=2 * count * responses * 512, bytes_accessed=count * responses, transcendentals=1024
        ),
    )(at, features, *chosen)


def swap(value, axis):
    return lax.ppermute(value, axis, [(0, 1), (1, 0)])


def in_order(index, mine, other):
    return jnp.where(index == 0, jnp.stack([mine, other]), jnp.stack([other, mine]))


def per_device(embeddings, landmarks, alpha, pairs):
    rows, pair_count = embeddings.shape[0], pairs.shape[1]
    planes = lax.axis_size(PLANE)
    slabs = lax.axis_size("zh")
    scale = 1.0 / math.sqrt(pair_count * slabs * planes)
    zh, zp = lax.axis_index("zh"), lax.axis_index("zp")

    sent = lax.dynamic_slice_in_dim(embeddings, (1 - zp) * (rows // 2), rows // 2)
    kept = lax.dynamic_slice_in_dim(embeddings, zp * (rows // 2), rows // 2)
    emb = lax.all_gather(in_order(zp, kept, swap(sent, "zp")), RING)
    emb = emb.reshape((-1,) + emb.shape[-2:])

    half = landmarks.shape[0] // slabs
    low, high = landmarks[:half], landmarks[half:]
    kept, sent = jnp.where(zh == 0, low, high), jnp.where(zh == 0, high, low)
    part = in_order(zh, kept, swap(sent, "zh")).transpose(1, 0, 2).reshape(half, -1)
    part = in_order(zp, part, swap(part, "zp")).reshape(2 * half, -1)
    land = lax.all_to_all(jnp.broadcast_to(part[None], (planes,) + part.shape), PLANE, 0, 0, tiled=True)

    own_alpha = jnp.where(zh == 0, alpha[:half], alpha[half:])
    own_alpha = in_order(zp, own_alpha, swap(own_alpha, "zp")).reshape(-1, 1)

    blocks = rows // BLOCK_ROWS
    local = pairs.reshape(2, blocks, -1) - BLOCK_ROWS * jnp.arange(blocks, dtype=pairs.dtype)[None, :, None]
    local = jnp.where(zp == 0, local[:, : blocks // 2], local[:, blocks // 2 :]).transpose(1, 0, 2)
    row_pairs = in_order(zh, local, swap(local, "zh")).reshape(blocks, 2, -1)
    col_pairs = row_pairs.transpose(0, 2, 1)

    mine, score = make_features(emb, land, make_norms(land), own_alpha, slabs)
    features = lax.all_gather(mine, RING, axis=0, tiled=True)
    ring = lax.axis_size(RING)
    scores = lax.all_to_all(jnp.broadcast_to(score, (ring, score.shape[1])), RING, 0, 0, tiled=True)
    at = jnp.stack([zh, lax.axis_index(("zm", "c"))]).astype(jnp.int32)
    chosen = make_pairs(scores, row_pairs, col_pairs, scale)
    parts = make_gram(at, features, chosen, 2 * planes)
    parts = lax.all_to_all(parts, PLANE + ("zp",), 0, 0, tiled=True)
    total = jnp.sum(parts.astype(jnp.float32), axis=0)
    gram = jnp.concatenate([total[:BLOCK_ROWS], total[BLOCK_ROWS : 2 * BLOCK_ROWS]], axis=1)
    tail = total[2 * BLOCK_ROWS :]
    return gram, jnp.concatenate([tail[0] + tail[2], tail[1] + tail[3]])


def solution(mesh):
    fine = Mesh(mesh.devices.reshape(4, 4, 2, 4, 2, 2), ("y", "x", "zh", "zm", "zp", "c"))
    dp, land = ("y", "x", "zh"), ("zm", "zp", "c")
    return jax.shard_map(
        per_device,
        mesh=fine,
        in_specs=(P(dp, land), P(land, dp), P(land), P(None, dp)),
        out_specs=(P(dp, land), P(land)),
        check_vma=False,
    )
```

```python
import functools
import math

import jax
import jax.numpy as jnp
from jax import lax
from jax.experimental import pallas as pl
from jax.experimental.pallas import tpu as pltpu
from jax.sharding import Mesh, PartitionSpec as P

EMBED_WIDTH = 4096
BLOCK_ROWS = 128
BETA = 0.5 * math.sqrt(EMBED_WIDTH)
RING = ("zh", "zm", "c")
PLANE = ("y", "x")
NT = (((1,), (1,)), ((), ()))


def norms_kernel(land_ref, out_ref):
    chunks, count, width = land_ref.shape
    total = jnp.zeros((count, 128), jnp.float32)
    for j in range(chunks):
        for lane in range(0, width, 128):
            part = land_ref[j, :, lane : lane + 128].astype(jnp.float32)
            total += part * part
    ones = jnp.ones((8, 128), jnp.float32)
    norm = lax.dot_general(ones, total, NT, precision=lax.Precision.HIGHEST, preferred_element_type=jnp.float32)
    out_ref[...] = lax.rsqrt(norm[0:1] + 1e-06)


def make_norms(land):
    return pl.pallas_call(
        norms_kernel,
        in_specs=[pl.BlockSpec(memory_space=pltpu.VMEM)],
        out_specs=pl.BlockSpec(memory_space=pltpu.VMEM),
        out_shape=jax.ShapeDtypeStruct((1, land.shape[1]), jnp.float32),
        compiler_params=pltpu.CompilerParams(vmem_limit_bytes=16 * 1024 * 1024),
        cost_estimate=pl.CostEstimate(flops=2 * land.size, bytes_accessed=2 * land.size, transcendentals=256),
    )(land)


def features_kernel(emb_ref, land_ref, norm_ref, alpha_ref, out_ref, score_ref):
    chunks, rows, width = emb_ref.shape
    count = land_ref.shape[1]
    total = jnp.zeros((rows, count), jnp.float32)
    resp = jnp.zeros((rows, 128), jnp.float32)
    for j in range(chunks):
        zm, c, zp = j // 4, j // 2 % 2, j % 2
        at = zm * 4 + zp * 2 + c
        total += lax.dot_general(emb_ref[j], land_ref[at], NT, preferred_element_type=jnp.float32)
        for lane in range(0, width, 128):
            part = emb_ref[j, :, lane : lane + 128].astype(jnp.float32)
            resp += part * part
    square = jnp.sum(resp, axis=1, keepdims=True)
    value = BETA * total * lax.rsqrt(square + 1e-06) * norm_ref[...]
    features = jnp.exp(value).T.astype(out_ref.dtype)
    out_ref[...] = features
    score_ref[...] = jnp.sum(features.astype(jnp.float32) * alpha_ref[...], axis=0, keepdims=True)


def make_features(emb, land, norms, alpha, slabs):
    chunks, rows, part = emb.shape
    count = land.shape[1]
    each = chunks // slabs
    return pl.pallas_call(
        features_kernel,
        grid=(slabs,),
        in_specs=[
            pl.BlockSpec((each, rows, part), lambda s: (s, 0, 0)),
            pl.BlockSpec(land.shape, lambda s: (0, 0, 0)),
            pl.BlockSpec((1, count), lambda s: (0, 0)),
            pl.BlockSpec((count, 1), lambda s: (0, 0)),
        ],
        out_specs=[
            pl.BlockSpec((count, rows), lambda s: (0, s)),
            pl.BlockSpec((1, rows), lambda s: (0, s)),
        ],
        out_shape=[
            jax.ShapeDtypeStruct((count, slabs * rows), jnp.bfloat16),
            jax.ShapeDtypeStruct((1, slabs * rows), jnp.float32),
        ],
        compiler_params=pltpu.CompilerParams(vmem_limit_bytes=60 * 1024 * 1024),
        cost_estimate=pl.CostEstimate(
            flops=2 * count * chunks * rows * part,
            bytes_accessed=2 * chunks * rows * part,
            transcendentals=count * slabs * rows,
        ),
    )(emb, land, norms, alpha)


def pairs_kernel(scale, score_ref, row_ref, col_ref, select_ref, back_ref, weight_ref, rest_ref):
    pairs = 2 * BLOCK_ROWS
    scores = jnp.sum(score_ref[...], axis=0, keepdims=True)
    lane = lax.broadcasted_iota(jnp.int32, (pairs, BLOCK_ROWS), 1)
    sub = lax.broadcasted_iota(jnp.int32, (BLOCK_ROWS, pairs), 0)
    for b in range(col_ref.shape[0]):
        cols = slice(b * BLOCK_ROWS, (b + 1) * BLOCK_ROWS)
        select = jnp.where(col_ref[b, :, 0:1] == lane, 1.0, 0.0) - jnp.where(col_ref[b, :, 1:2] == lane, 1.0, 0.0)
        margin = jnp.sum(select * scores[:, cols], axis=1, keepdims=True)
        prob = 1.0 / (1.0 + jnp.exp(-margin))
        weight_ref[b] = prob * (1.0 - prob) * scale
        rest_ref[b] = (1.0 - prob) * scale
        select_ref[b] = select.astype(jnp.bfloat16)
        back = jnp.where(row_ref[b, 0:1, :] == sub, 1.0, 0.0) - jnp.where(row_ref[b, 1:2, :] == sub, 1.0, 0.0)
        back_ref[b] = back.astype(jnp.bfloat16)


def make_pairs(scores, row_pairs, col_pairs, scale):
    blocks, _, pairs = row_pairs.shape
    vmem = pl.BlockSpec(memory_space=pltpu.VMEM)
    return pl.pallas_call(
        functools.partial(pairs_kernel, scale),
        in_specs=[vmem] * 3,
        out_specs=[vmem] * 4,
        out_shape=[
            jax.ShapeDtypeStruct((blocks, pairs, BLOCK_ROWS), jnp.bfloat16),
            jax.ShapeDtypeStruct((blocks, BLOCK_ROWS, pairs), jnp.bfloat16),
            jax.ShapeDtypeStruct((blocks, pairs, 1), jnp.float32),
            jax.ShapeDtypeStruct((blocks, pairs, 1), jnp.float32),
        ],
        compiler_params=pltpu.CompilerParams(vmem_limit_bytes=16 * 1024 * 1024),
        cost_estimate=pl.CostEstimate(flops=1000000, bytes_accessed=2000000, transcendentals=1024),
    )(scores, row_pairs, col_pairs)


def gram_kernel(
    at_ref, feat_ref, select_ref, back_ref, weight_ref, rest_ref, out_ref, own_ref, half_ref, v_ref, sems
):
    half, own = at_ref[0], at_ref[1]
    count, responses = feat_ref.shape
    blocks = responses // BLOCK_ROWS
    pairs = 2 * BLOCK_ROWS
    wide = 4 * BLOCK_ROWS
    copies = []
    for zh in range(2):
        rows = pl.ds(pl.multiple_of(zh * (count // 2) + own * pairs, BLOCK_ROWS), pairs)
        copies.append(pltpu.make_async_copy(feat_ref.at[rows], own_ref.at[pl.ds(zh * pairs, pairs)], sems.at[zh]))
    rows = pl.ds(pl.multiple_of(half * (count // 2), BLOCK_ROWS), count // 2)
    copies.append(pltpu.make_async_copy(feat_ref.at[rows], half_ref, sems.at[2]))
    for copy in copies:
        copy.start()
    for copy in copies[:2]:
        copy.wait()

    grad = jnp.zeros((1, wide), jnp.float32)
    for b in range(blocks):
        cols = slice(b * BLOCK_ROWS, (b + 1) * BLOCK_ROWS)
        diffs = lax.dot_general(select_ref[b], own_ref[:, cols], NT, preferred_element_type=jnp.float32)
        diffs = diffs.astype(jnp.bfloat16).astype(jnp.float32)
        weighted = (diffs * weight_ref[b]).astype(jnp.bfloat16)
        grad += jnp.sum(diffs * rest_ref[b], axis=0, keepdims=True)
        v = jnp.dot(back_ref[b], weighted, preferred_element_type=jnp.float32)
        v_high = v.astype(jnp.bfloat16)
        v_ref[cols, 0:wide] = v_high
        v_ref[cols, wide : 2 * wide] = (v - v_high.astype(jnp.float32)).astype(jnp.bfloat16)

    high = grad.astype(jnp.bfloat16).astype(jnp.float32)
    low = grad - high
    row = lax.broadcasted_iota(jnp.int32, (16, BLOCK_ROWS), 0)
    tails = []
    for k in range(2):
        left = slice(k * BLOCK_ROWS, (k + 1) * BLOCK_ROWS)
        right = slice((k + 2) * BLOCK_ROWS, (k + 3) * BLOCK_ROWS)
        tail = jnp.zeros((16, BLOCK_ROWS), jnp.float32)
        for at, value in enumerate((high[:, left], high[:, right], low[:, left], low[:, right])):
            tail = jnp.where(row == at, value, tail)
        tails.append(tail.astype(jnp.bfloat16))
    copies[2].wait()
    group = 16
    for start in range(0, count // 2 // BLOCK_ROWS, group):
        part = jnp.dot(
            half_ref[start * BLOCK_ROWS : (start + group) * BLOCK_ROWS, :],
            v_ref[...],
            preferred_element_type=jnp.float32,
        )
        part = (part[:, 0:wide] + part[:, wide:]).astype(jnp.bfloat16)
        for e in range(start, start + group):
            d = e // 4 * 4 + e % 2 * 2 + e // 2 % 2
            rows = slice((e - start) * BLOCK_ROWS, (e - start + 1) * BLOCK_ROWS)
            for k in range(2):
                for side in range(2):
                    at = (2 * side + k) * BLOCK_ROWS
                    out_ref[2 * d + k, side * BLOCK_ROWS : (side + 1) * BLOCK_ROWS, :] = part[
                        rows, at : at + BLOCK_ROWS
                    ]
                out_ref[2 * d + k, 2 * BLOCK_ROWS :, :] = tails[k]


def make_gram(at, features, chosen, owners):
    count, responses = features.shape
    vmem = pl.BlockSpec(memory_space=pltpu.VMEM)
    return pl.pallas_call(
        gram_kernel,
        in_specs=[
            pl.BlockSpec(memory_space=pltpu.SMEM),
            pl.BlockSpec(memory_space=pl.ANY),
            vmem,
            vmem,
            vmem,
            vmem,
        ],
        out_specs=vmem,
        out_shape=jax.ShapeDtypeStruct((owners, 2 * BLOCK_ROWS + 16, BLOCK_ROWS), jnp.bfloat16),
        scratch_shapes=[
            pltpu.VMEM((4 * BLOCK_ROWS, responses), jnp.bfloat16),
            pltpu.VMEM((count // 2, responses), jnp.bfloat16),
            pltpu.VMEM((responses, 8 * BLOCK_ROWS), jnp.bfloat16),
            pltpu.SemaphoreType.DMA((3,)),
        ],
        compiler_params=pltpu.CompilerParams(vmem_limit_bytes=50 * 1024 * 1024),
        cost_estimate=pl.CostEstimate(
            flops=2 * count * responses * 512, bytes_accessed=count * responses, transcendentals=1024
        ),
    )(at, features, *chosen)


def swap(value, axis):
    return lax.ppermute(value, axis, [(0, 1), (1, 0)])


def in_order(index, mine, other):
    return jnp.where(index == 0, jnp.stack([mine, other]), jnp.stack([other, mine]))


def per_device(embeddings, landmarks, alpha, pairs):
    rows, pair_count = embeddings.shape[0], pairs.shape[1]
    planes = lax.axis_size(PLANE)
    slabs = lax.axis_size("zh")
    scale = 1.0 / math.sqrt(pair_count * slabs * planes)
    zh, zp = lax.axis_index("zh"), lax.axis_index("zp")

    sent = lax.dynamic_slice_in_dim(embeddings, (1 - zp) * (rows // 2), rows // 2)
    kept = lax.dynamic_slice_in_dim(embeddings, zp * (rows // 2), rows // 2)
    emb = lax.all_gather(in_order(zp, kept, swap(sent, "zp")), RING)
    emb = emb.reshape((-1,) + emb.shape[-2:])

    half = landmarks.shape[0] // slabs
    low, high = landmarks[:half], landmarks[half:]
    kept, sent = jnp.where(zh == 0, low, high), jnp.where(zh == 0, high, low)
    part = in_order(zh, kept, swap(sent, "zh")).transpose(1, 0, 2).reshape(half, -1)
    part = in_order(zp, part, swap(part, "zp")).reshape(2 * half, -1)
    land = lax.all_to_all(jnp.broadcast_to(part[None], (planes,) + part.shape), PLANE, 0, 0, tiled=True)

    own_alpha = jnp.where(zh == 0, alpha[:half], alpha[half:])
    own_alpha = in_order(zp, own_alpha, swap(own_alpha, "zp")).reshape(-1, 1)

    blocks = rows // BLOCK_ROWS
    local = pairs.reshape(2, blocks, -1) - BLOCK_ROWS * jnp.arange(blocks, dtype=pairs.dtype)[None, :, None]
    local = jnp.where(zp == 0, local[:, : blocks // 2], local[:, blocks // 2 :]).transpose(1, 0, 2)
    row_pairs = in_order(zh, local, swap(local, "zh")).reshape(blocks, 2, -1)
    col_pairs = row_pairs.transpose(0, 2, 1)

    mine, score = make_features(emb, land, make_norms(land), own_alpha, slabs)
    features = lax.all_gather(mine, RING, axis=0, tiled=True)
    ring = lax.axis_size(RING)
    scores = lax.all_to_all(jnp.broadcast_to(score, (ring, score.shape[1])), RING, 0, 0, tiled=True)
    at = jnp.stack([zh, lax.axis_index(("zm", "c"))]).astype(jnp.int32)
    chosen = make_pairs(scores, row_pairs, col_pairs, scale)
    parts = make_gram(at, features, chosen, 2 * planes)
    parts = lax.all_to_all(parts, PLANE + ("zp",), 0, 0, tiled=True)
    total = jnp.sum(parts.astype(jnp.float32), axis=0)
    gram = jnp.concatenate([total[:BLOCK_ROWS], total[BLOCK_ROWS : 2 * BLOCK_ROWS]], axis=1)
    tail = total[2 * BLOCK_ROWS :]
    return gram, jnp.concatenate([tail[0] + tail[2], tail[1] + tail[3]])


def solution(mesh):
    fine = Mesh(mesh.devices.reshape(4, 4, 2, 4, 2, 2), ("y", "x", "zh", "zm", "zp", "c"))
    dp, land = ("y", "x", "zh"), ("zm", "zp", "c")
    return jax.shard_map(
        per_device,
        mesh=fine,
        in_specs=(P(dp, land), P(land, dp), P(land), P(None, dp)),
        out_specs=(P(dp, land), P(land)),
        check_vma=False,
    )
```
